256 devices in a mesh: dp: 4 (over z_hi), seq: 64 (over x, z_lo, y, core).
Axes of the slice: x: 4, y: 4, z: 8 (z_hi: 4, z_lo: 2; z = z_hi * 2 + z_lo), core: 2. Of those that a mesh axis runs over, the one named last changes fastest.
Arguments:
- inputs: bfloat16 [12, 16384, 768], P('dp', 'seq'), may hold values from -6 to 6
- dilated_tap_weight: bfloat16 [3, 768, 384], replicated, may hold values from -0.125 to 0.125
- proj_weight: bfloat16 [384, 768], replicated, may hold values from -0.3125 to 0.3125
- cotangent: bfloat16 [12, 16384, 768], P('dp', 'seq'), may hold values from -6 to 6
Outputs:
- block_out: bfloat16 [12, 16384, 768], P('dp', 'seq')
- input_grad: bfloat16 [12, 16384, 768], P('dp', 'seq')
- conv_grad: float32 [6912, 128], P(('dp', 'seq'))
- proj_grad: float32 [2304, 128], P(('dp', 'seq'))
The draws below stay inside these ranges and needn't reach their ends.
All inputs are finite; a program needn't handle non-finite values.
Results may differ from the reference program's by a relative error of at most 0.0054.
Values may be sent and summed in bfloat16 or wider, within the bound.
A program may use at most 64 MiB of HBM per device.

```python
import math
import jax
import jax.numpy as jnp
from jax import lax

C = 768
BN = 384
DILATION_BINS = 512
WINDOWS = 12
SEQ_LEN = 16384


def block_scale(own_key, dims, shards, low, top_value):
    factor_of = 1.0
    for axis_at, blocks in shards:
        draws = jax.random.uniform(jax.random.fold_in(jax.random.fold_in(own_key, 6), axis_at), (blocks,), jnp.float32, low / len(shards), top_value / len(shards))
        factor_of = factor_of * jnp.repeat(jnp.exp(draws), dims[axis_at] // blocks).reshape((-1,) + (1,) * (len(dims) - 1 - axis_at))
    return factor_of


def gaussian(rng, shape, deviation, bound, pieces=(), held_as=jnp.bfloat16):
    array = deviation * jax.random.normal(rng, shape, jnp.float32)
    if pieces:
        array = array * block_scale(rng, shape, pieces, -0.22, 0.18)
    return jnp.clip(array, -bound, bound).astype(held_as)


def setup_inputs(seed: int = 0) -> dict:
    keys = jax.random.split(jax.random.key(seed), 5)
    inputs = gaussian(keys[0], (WINDOWS, SEQ_LEN, C), 1.0, 6.0, ((0, 4), (1, 64)))
    dilated_tap_weight = gaussian(keys[1], (3, C, BN), (3 * C) ** -0.5, 0.125)
    proj_weight = gaussian(keys[2], (BN, C), BN ** -0.5, 0.3125)
    cotangent = gaussian(keys[3], (WINDOWS, SEQ_LEN, C), 1.0, 6.0, ((0, 4), (1, 64)))
    return dict(inputs=inputs, dilated_tap_weight=dilated_tap_weight, proj_weight=proj_weight, cotangent=cotangent)


def neighbour_rows(values, rows):
    zeros = jnp.zeros((abs(rows), values.shape[1]), values.dtype)
    if rows > 0:
        return jnp.concatenate([zeros, values[:values.shape[0] - rows]], axis=0)
    return jnp.concatenate([values[-rows:], zeros], axis=0)

def reference(inputs, dilated_tap_weight, proj_weight, cotangent):

    def one_window(carry, pair):
        x_win, g_win = pair
        x_f = x_win.astype(jnp.float32)
        act_f, act_back = jax.vjp(jax.nn.gelu, x_f)
        gelu_activation = act_f.astype(jnp.bfloat16)
        kernel_taps = (neighbour_rows(gelu_activation, DILATION_BINS), gelu_activation, neighbour_rows(gelu_activation, -DILATION_BINS))
        pre = jnp.dot(kernel_taps[0], dilated_tap_weight[0], preferred_element_type=jnp.float32)
        pre = pre + jnp.dot(kernel_taps[1], dilated_tap_weight[1], preferred_element_type=jnp.float32)
        pre = pre + jnp.dot(kernel_taps[2], dilated_tap_weight[2], preferred_element_type=jnp.float32)
        mid_f, mid_back = jax.vjp(jax.nn.gelu, pre)
        mid = mid_f.astype(jnp.bfloat16)
        out = (x_f + jnp.dot(mid, proj_weight, preferred_element_type=jnp.float32)).astype(jnp.bfloat16)
        d_mid = jnp.dot(g_win, proj_weight.T, preferred_element_type=jnp.float32)
        preactivation_gradient = mid_back(d_mid)[0].astype(jnp.bfloat16)
        proj_term = jnp.dot(mid.T, g_win, preferred_element_type=jnp.float32)
        conv_term = jnp.stack([jnp.dot(tap.T, preactivation_gradient, preferred_element_type=jnp.float32) for tap in kernel_taps])
        activation_gradient = jnp.dot(neighbour_rows(preactivation_gradient, -DILATION_BINS), dilated_tap_weight[0].T, preferred_element_type=jnp.float32)
        activation_gradient = activation_gradient + jnp.dot(preactivation_gradient, dilated_tap_weight[1].T, preferred_element_type=jnp.float32)
        activation_gradient = activation_gradient + jnp.dot(neighbour_rows(preactivation_gradient, DILATION_BINS), dilated_tap_weight[2].T, preferred_element_type=jnp.float32)
        d_x = (g_win.astype(jnp.float32) + act_back(activation_gradient)[0]).astype(jnp.bfloat16)
        return ((carry[0] + conv_term, carry[1] + proj_term), (out, d_x))
    start = (jnp.zeros((3, C, BN), jnp.float32), jnp.zeros((BN, C), jnp.float32))
    sums, outputs = lax.scan(one_window, start, (inputs, cotangent))
    factor = 1.0 / math.sqrt(WINDOWS * SEQ_LEN)
    conv_grad = (sums[0] * factor).reshape(-1, 128)
    proj_grad = (sums[1] * factor).reshape(-1, 128)
    return (outputs[0], outputs[1], conv_grad, proj_grad)
```

```python
import functools
import math

import jax
import jax.numpy as jnp
from jax import lax
from jax.experimental import pallas as pl
from jax.experimental.pallas import tpu as pltpu
from jax.sharding import PartitionSpec as P

MESH = pl.DeviceIdType.MESH
F32 = jnp.float32
BF16 = jnp.bfloat16
SLOPE = math.sqrt(2.0 / math.pi)
CUBIC = 0.044715

WIN = 3
BINS = 256
ROWS = WIN * BINS
C = 768
BN = 384
COL = 128
CHUNKS = BN // COL
PROJ = CHUNKS
ROUNDS = CHUNKS + 1
ALL = 2304
UNIT = 72
PART = 4 * UNIT
OWN = 9


def gelu_parts(v):
    sq = v * v
    t = jnp.tanh(SLOPE * v * (1.0 + CUBIC * sq))
    half = 0.5 * (1.0 + t)
    value = v * half
    slope = half + (0.5 * SLOPE) * v * (1.0 - t * t) * (1.0 + (3.0 * CUBIC) * sq)
    return value, slope


def dot(a, b, ca=1, cb=0):
    return lax.dot_general(a, b, (((ca,), (cb,)), ((), ())), preferred_element_type=F32)


def kernel(
    factor,
    x_hbm, w_hbm, p_hbm, g_hbm,
    out_hbm, dx_hbm, conv_ref, proj_ref,
    x_v, w_v, p_v, g_v, act, act_t, slope_x, cpre, dmid, mid, dact, out_v, dx_v,
    u_send, v_send, u_recv, v_recv, d_send, dup_recv, dlo_recv,
    total, pair_send, pair_recv, x_send, x_recv, acc, yz_send, yz_recv,
    in_sem, out_sem, ph_send_sem, u_sem, v_sem, dup_sem, dlo_sem,
    pair_ssem, pair_rsem, x_ssem, x_rsem, yz_ssem, yz_rsem,
):
    zh = lax.axis_index("dp")
    s = lax.axis_index("seq")
    x = s // 16
    zl = lax.rem(s // 8, 2)
    y = lax.rem(s // 2, 4)
    c = lax.rem(s, 2)
    off = lax.rem(zl + c, 2)

    def device(zh_, x_, zl_, y_, c_):
        return (zh_, ((x_ * 2 + zl_) * 4 + y_) * 2 + c_)

    upper = (zh, lax.rem(s + 2, 64))
    lower = (zh, lax.rem(s + 62, 64))
    sibling = device(zh, x, zl, y, 1 - c)

    loads = {}
    def load(name, src, dst, i):
        loads[name] = pltpu.make_async_copy(src, dst, in_sem.at[i])
        loads[name].start()
    load("x0", x_hbm.at[0], x_v.at[0], 0)
    load("w0", w_hbm.at[0], w_v.at[0], 3)
    load("w2", w_hbm.at[2], w_v.at[2], 5)
    load("x1", x_hbm.at[1], x_v.at[1], 1)
    load("x2", x_hbm.at[2], x_v.at[2], 2)
    load("w1", w_hbm.at[1], w_v.at[1], 4)
    load("p", p_hbm, p_v, 6)
    load("g", g_hbm, g_v, 7)

    barrier = pltpu.get_barrier_semaphore()
    def greet(peer):
        pl.semaphore_signal(barrier, inc=1, device_id=peer, device_id_type=MESH)
    greet(upper)
    greet(lower)
    greet(sibling)
    for k in (1, 2, 3):
        greet(device(zh, lax.rem(x + k, 4), zl, y, c))
    for kz in range(4):
        for ky in range(4):
            for kl in range(2):
                peer = device(lax.rem(zh + kz, 4), x, lax.rem(zl + c + kl, 2), lax.rem(y + ky, 4), zl)
                if kz == 0 and ky == 0 and kl == 0:
                    pass
                me_too = (kz == 0 and ky == 0)
                if me_too:
                    is_self = jnp.logical_and(lax.rem(zl + c + kl, 2) == zl, c == zl)
                    @pl.when(jnp.logical_not(is_self))
                    def _(peer=peer):
                        greet(peer)
                else:
                    greet(peer)

    n_far = jnp.where(off == 0, 31, 32)

    def send_halo(src, dst, sem, ssem, ch, w, to):
        pltpu.make_async_remote_copy(
            src_ref=src.at[ch, pl.ds(w * BINS, BINS)],
            dst_ref=dst.at[ch, pl.ds(w * BINS, BINS)],
            send_sem=ph_send_sem.at[ssem],
            recv_sem=sem.at[ch, w],
            device_id=to,
            device_id_type=MESH,
        ).start()

    def wait_halo(dst, sem, ch, w):
        ref = dst.at[ch, pl.ds(w * BINS, BINS)]
        pltpu.make_async_remote_copy(
            src_ref=ref, dst_ref=ref, send_sem=ph_send_sem.at[0], recv_sem=sem.at[ch, w],
            device_id=upper, device_id_type=MESH,
        ).wait_recv()

    SLAB = 16
    for w in range(WIN):
        loads["x%d" % w].wait()
        def activate(i, carry, w=w):
            r = pl.multiple_of(i * SLAB, SLAB)
            v = x_v[w, pl.ds(r, SLAB), :].astype(F32)
            value, slope = gelu_parts(v)
            act[pl.ds(w * BINS + r, SLAB), :] = value.astype(BF16)
            slope_x[pl.ds(w * BINS + r, SLAB), :] = slope
            return carry
        lax.fori_loop(0, BINS // SLAB, activate, 0)
        a_w = act[pl.ds(w * BINS, BINS), :]
        if w == 0:
            loads["w0"].wait()
        u = dot(a_w, w_v[0]).astype(BF16)
        for ch in range(CHUNKS):
            u_send[ch, pl.ds(w * BINS, BINS), :] = u[:, ch * COL:(ch + 1) * COL]
        if w == 0:
            pl.semaphore_wait(barrier, 2 + 1 + 3 + n_far)
        send_halo(u_send, u_recv, u_sem, 0, 0, w, upper)
        if w == 0:
            loads["w2"].wait()
        v = dot(a_w, w_v[2]).astype(BF16)
        for ch in range(CHUNKS):
            v_send[ch, pl.ds(w * BINS, BINS), :] = v[:, ch * COL:(ch + 1) * COL]
        send_halo(v_send, v_recv, v_sem, 1, 0, w, lower)
    for ch in range(1, CHUNKS):
        for w in range(WIN):
            send_halo(u_send, u_recv, u_sem, 0, ch, w, upper)
            send_halo(v_send, v_recv, v_sem, 1, ch, w, lower)

    loads["w1"].wait()
    loads["p"].wait()
    loads["g"].wait()
    for w in range(WIN):
        rows = pl.ds(w * BINS, BINS)
        cpre[rows, :] = dot(act[rows, :], w_v[1])
        dmid[rows, :] = dot(g_v[w], p_v[...], 1, 1)
        act_t[:, rows] = act[rows, :].T

    def clear_if(cond, ref, ch, w):
        @pl.when(cond)
        def _():
            ref[ch, pl.ds(w * BINS, BINS), :] = jnp.zeros((BINS, COL), BF16)

    MIDSLAB = 64
    for ch in range(CHUNKS):
        for w in range(WIN):
            wait_halo(u_recv, u_sem, ch, w)
            wait_halo(v_recv, v_sem, ch, w)
            clear_if(s < 2, u_recv, ch, w)
            clear_if(s >= 62, v_recv, ch, w)
            def bottleneck(i, carry, ch=ch, w=w):
                r = pl.multiple_of(w * BINS + i * MIDSLAB, MIDSLAB)
                rows = pl.ds(r, MIDSLAB)
                cols = pl.ds(ch * COL, COL)
                pre = cpre[rows, cols] + u_recv[ch, rows, :].astype(F32) + v_recv[ch, rows, :].astype(F32)
                value, slope = gelu_parts(pre)
                mid[rows, cols] = value.astype(BF16)
                d_send[ch, rows, :] = (dmid[rows, cols] * slope).astype(BF16)
                return carry
            lax.fori_loop(0, BINS // MIDSLAB, bottleneck, 0)
            send_halo(d_send, dlo_recv, dlo_sem, 2, ch, w, upper)
            send_halo(d_send, dup_recv, dup_sem, 3, ch, w, lower)
        total[ch, pl.ds(C, C), :] = dot(act_t[...], d_send[ch])

    def unit(rnd, zh_, x_, zl_):
        start = pl.multiple_of((zh_ * 8 + x_ * 2 + zl_) * UNIT, 8)
        return total[rnd, pl.ds(start, UNIT), :]

    def part(rnd, x_, zl_):
        return jnp.concatenate([unit(rnd, k, x_, zl_) for k in range(4)], axis=0)

    def pair_copy(rnd):
        return pltpu.make_async_remote_copy(
            src_ref=pair_send.at[rnd], dst_ref=pair_recv.at[rnd],
            send_sem=pair_ssem.at[rnd], recv_sem=pair_rsem.at[rnd],
            device_id=sibling, device_id_type=MESH,
        )

    def stage_a(rnd):
        for xa in range(4):
            pair_send[rnd, pl.ds(xa * PART, PART), :] = part(rnd, xa, 1 - c).astype(BF16)
        pair_copy(rnd).start()

    def x_copy(rnd, k):
        return pltpu.make_async_remote_copy(
            src_ref=x_send.at[rnd, k - 1], dst_ref=x_recv.at[rnd, k - 1],
            send_sem=x_ssem.at[rnd, k - 1], recv_sem=x_rsem.at[rnd, k - 1],
            device_id=device(zh, lax.rem(x + k, 4), zl, y, c), device_id_type=MESH,
        )

    def stage_b(rnd):
        pair_copy(rnd).wait_recv()
        for k in (2, 1, 3, 0):
            xa = lax.rem(x + k, 4)
            other = pair_recv[rnd, pl.ds(pl.multiple_of(xa * PART, 16), PART), :]
            both = part(rnd, xa, c) + other.astype(F32)
            if k:
                x_send[rnd, k - 1] = both.astype(BF16)
                x_copy(rnd, k).start()
            else:
                acc[rnd, pl.ds(0, PART), :] = both
                acc[rnd, pl.ds(PART, 16), :] = jnp.zeros((16, COL), F32)

    def far_copy(rnd, kz, ky, kc):
        za = lax.rem(zh + kz, 4)
        ya = lax.rem(y + ky, 4)
        ca = lax.rem(c + kc, 2)
        return pltpu.make_async_remote_copy(
            src_ref=yz_send.at[rnd, (za * 4 + ya) * 2 + ca],
            dst_ref=yz_recv.at[rnd, (kz * 4 + ky) * 2 + off],
            send_sem=yz_ssem.at[rnd], recv_sem=yz_rsem.at[rnd],
            device_id=device(za, x, c, ya, ca), device_id_type=MESH,
        )

    def stage_c(rnd):
        for k in (1, 3, 2):
            x_copy(rnd, k).wait_recv()
        acc[rnd, pl.ds(0, PART), :] = (
            acc[rnd, pl.ds(0, PART), :] + x_recv[rnd, 0].astype(F32)
            + x_recv[rnd, 1].astype(F32) + x_recv[rnd, 2].astype(F32)
        )
        for b in range(32):
            yz_send[rnd, b] = acc[rnd, pl.ds(OWN * b, 16), :].astype(BF16)
        for kz in (2, 1, 3, 0):
            for ky in (2, 1, 3, 0):
                for kc in (1, 0):
                    if kz == 0 and ky == 0 and kc == 0:
                        @pl.when(off == 0)
                        def _():
                            yz_recv[rnd, 0] = yz_send[rnd, (zh * 4 + y) * 2 + c]
                        @pl.when(off == 1)
                        def _():
                            far_copy(rnd, 0, 0, 0).start()
                    else:
                        far_copy(rnd, kz, ky, kc).start()

    def far_wait(rnd, first, recv):
        ref = yz_recv.at[rnd, pl.ds(first, 32 - first)]
        copy = pltpu.make_async_remote_copy(
            src_ref=yz_send.at[rnd, pl.ds(first, 32 - first)], dst_ref=ref,
            send_sem=yz_ssem.at[rnd], recv_sem=yz_rsem.at[rnd],
            device_id=sibling, device_id_type=MESH,
        )
        if recv:
            copy.wait_recv()
        else:
            copy.wait_send()

    def far_wait_all(rnd, recv):
        @pl.when(off == 0)
        def _():
            far_wait(rnd, 1, recv)
        @pl.when(off == 1)
        def _():
            far_wait(rnd, 0, recv)

    def stage_d(rnd):
        far_wait_all(rnd, True)
        result = jnp.sum(yz_recv[rnd].astype(F32), axis=0)[:OWN] * factor
        if rnd == PROJ:
            proj_ref[...] = result
        else:
            conv_ref[pl.ds(rnd, OWN, stride=CHUNKS), :] = result

    grad = dot(mid[pl.ds(0, BINS), :], g_v[0], 0, 0)
    for w in range(1, WIN):
        grad = grad + dot(mid[pl.ds(w * BINS, BINS), :], g_v[w], 0, 0)
    for j in range(C // COL):
        total[PROJ, pl.ds(j, BN, stride=C // COL), :] = grad[:, j * COL:(j + 1) * COL]
    stage_a(PROJ)
    stores = []
    for w in range(WIN):
        rows = pl.ds(w * BINS, BINS)
        out_v[w] = (x_v[w].astype(F32) + dot(mid[rows, :], p_v[...])).astype(BF16)
    stores.append(pltpu.make_async_copy(out_v, out_hbm, out_sem.at[0]))
    stores[0].start()
    stage_b(PROJ)

    def outer_taps(ch):
        for w in range(WIN):
            wait_halo(dup_recv, dup_sem, ch, w)
            wait_halo(dlo_recv, dlo_sem, ch, w)
            clear_if(s < 2, dlo_recv, ch, w)
            clear_if(s >= 62, dup_recv, ch, w)
        total[ch, pl.ds(0, C), :] = dot(act_t[...], dup_recv[ch])
        total[ch, pl.ds(2 * C, C), :] = dot(act_t[...], dlo_recv[ch])

    def input_side(ch):
        cols = pl.ds(ch * COL, COL)
        for w in range(WIN):
            rows = pl.ds(w * BINS, BINS)
            term = (
                dot(dup_recv[ch, rows, :], w_v[0, :, cols], 1, 1)
                + dot(d_send[ch, rows, :], w_v[1, :, cols], 1, 1)
                + dot(dlo_recv[ch, rows, :], w_v[2, :, cols], 1, 1)
            )
            if ch:
                term = term + dact[rows, :]
            if ch < CHUNKS - 1:
                dact[rows, :] = term
            else:
                dx_v[w] = (g_v[w].astype(F32) + term * slope_x[rows, :]).astype(BF16)

    outer_taps(0)
    stage_a(0)
    stage_c(PROJ)
    input_side(0)
    stage_b(0)
    outer_taps(1)
    stage_a(1)
    stage_c(0)
    stage_d(PROJ)
    input_side(1)
    stage_b(1)
    outer_taps(2)
    stage_a(2)
    stage_c(1)
    stage_b(2)
    input_side(2)
    stores.append(pltpu.make_async_copy(dx_v, dx_hbm, out_sem.at[1]))
    stores[1].start()
    stage_d(0)
    stage_c(2)
    stage_d(1)

    for i, (ref, to) in enumerate(((u_send, upper), (v_send, lower), (d_send, upper), (d_send, lower))):
        pltpu.make_async_remote_copy(
            src_ref=ref, dst_ref=ref, send_sem=ph_send_sem.at[i], recv_sem=u_sem.at[0, 0],
            device_id=to, device_id_type=MESH,
        ).wait_send()
    for rnd in range(ROUNDS):
        pair_copy(rnd).wait_send()
        for k in (1, 2, 3):
            x_copy(rnd, k).wait_send()
        far_wait_all(rnd, False)
    stage_d(2)
    for copy in stores:
        copy.wait()


def local(inputs, dilated_tap_weight, proj_weight, cotangent):
    total_rows = inputs.shape[0] * lax.axis_size("dp") * inputs.shape[1] * lax.axis_size("seq")
    factor = 1.0 / math.sqrt(total_rows)
    vm = pltpu.VMEM
    dma = pltpu.SemaphoreType.DMA
    halo = (CHUNKS, ROWS, COL)
    hbm = pl.BlockSpec(memory_space=pl.ANY)
    vmem = pl.BlockSpec(memory_space=pltpu.VMEM)
    return pl.pallas_call(
        functools.partial(kernel, factor),
        out_shape=(
            jax.ShapeDtypeStruct(inputs.shape, BF16),
            jax.ShapeDtypeStruct(inputs.shape, BF16),
            jax.ShapeDtypeStruct((CHUNKS * OWN, COL), F32),
            jax.ShapeDtypeStruct((OWN, COL), F32),
        ),
        in_specs=[hbm] * 4,
        out_specs=(hbm, hbm, vmem, vmem),
        scratch_shapes=[
            vm((WIN, BINS, C), BF16), vm((3, C, BN), BF16), vm((BN, C), BF16), vm((WIN, BINS, C), BF16),
            vm((ROWS, C), BF16), vm((C, ROWS), BF16), vm((ROWS, C), F32),
            vm((ROWS, BN), F32), vm((ROWS, BN), F32), vm((ROWS, BN), BF16), vm((ROWS, C), F32),
            vm((WIN, BINS, C), BF16), vm((WIN, BINS, C), BF16),
            vm(halo, BF16), vm(halo, BF16), vm(halo, BF16), vm(halo, BF16),
            vm(halo, BF16), vm(halo, BF16), vm(halo, BF16),
            vm((ROUNDS, ALL, COL), F32),
            vm((ROUNDS, 4 * PART, COL), BF16), vm((ROUNDS, 4 * PART, COL), BF16),
            vm((ROUNDS, 3, PART, COL), BF16), vm((ROUNDS, 3, PART, COL), BF16),
            vm((ROUNDS, PART + 16, COL), F32),
            vm((ROUNDS, 32, 16, COL), BF16), vm((ROUNDS, 32, 16, COL), BF16),
            dma((8,)), dma((2,)), dma((4,)),
            dma((CHUNKS, WIN)), dma((CHUNKS, WIN)), dma((CHUNKS, WIN)), dma((CHUNKS, WIN)),
            dma((ROUNDS,)), dma((ROUNDS,)), dma((ROUNDS, 3)), dma((ROUNDS, 3)),
            dma((ROUNDS,)), dma((ROUNDS,)),
        ],
        compiler_params=pltpu.CompilerParams(
            collective_id=0, has_side_effects=True, vmem_limit_bytes=56 * 1024 * 1024
        ),
        name="block",
    )(inputs, dilated_tap_weight, proj_weight, cotangent)


def solution(mesh):
    return jax.shard_map(
        local,
        mesh=mesh,
        in_specs=(P("dp", "seq", None), P(), P(), P("dp", "seq", None)),
        out_specs=(
            P("dp", "seq", None),
            P("dp", "seq", None),
            P(("dp", "seq"), None),
            P(("dp", "seq"), None),
        ),
        check_vma=False,
    )
```

```python
import functools
import math

import jax
import jax.numpy as jnp
from jax import lax
from jax.experimental import pallas as pl
from jax.experimental.pallas import tpu as pltpu
from jax.sharding import PartitionSpec as P

MESH = pl.DeviceIdType.MESH
F32 = jnp.float32
BF16 = jnp.bfloat16
SLOPE = math.sqrt(2.0 / math.pi)
CUBIC = 0.044715

WIN = 3
BINS = 256
ROWS = WIN * BINS
C = 768
BN = 384
COL = 128
CHUNKS = BN // COL
PROJ = CHUNKS
ROUNDS = CHUNKS + 1
LAST = CHUNKS - 1
ALL = 2304
UNIT = 72
PART = 4 * UNIT
LINE = 18
OWN = 9


def gelu_parts(v):
    sq = v * v
    t = jnp.tanh(SLOPE * v * (1.0 + CUBIC * sq))
    half = 0.5 * (1.0 + t)
    value = v * half
    slope = half + (0.5 * SLOPE) * v * (1.0 - t * t) * (1.0 + (3.0 * CUBIC) * sq)
    return value, slope


def dot(a, b, ca=1, cb=0):
    return lax.dot_general(a, b, (((ca,), (cb,)), ((), ())), preferred_element_type=F32)


def kernel(
    factor,
    x_hbm, w_hbm, p_hbm, g_hbm,
    out_hbm, dx_hbm, conv_ref, proj_ref,
    x_v, w_v, p_v, g_v, act, act_t, slope_x, cpre, dmid, mid, dact, out_v, dx_v,
    u_send, v_send, u_recv, v_recv, d_send, dup_recv, dlo_recv,
    total, pair_send, pair_recv, x_send, x_recv, acc,
    y_sum, y_send, y_recv, z_sum, z_send, z_recv,
    in_sem, out_sem, ph_send_sem, u_sem, v_sem, dup_sem, dlo_sem,
    pair_ssem, pair_rsem, x_ssem, x_rsem, y_ssem, y_rsem, z_ssem, z_rsem,
):
    zh = lax.axis_index("dp")
    s = lax.axis_index("seq")
    x = s // 16
    zl = lax.rem(s // 8, 2)
    y = lax.rem(s // 2, 4)
    c = lax.rem(s, 2)
    off = lax.rem(zl + c, 2)

    def device(zh_, x_, zl_, y_, c_):
        return (zh_, ((x_ * 2 + zl_) * 4 + y_) * 2 + c_)

    upper = (zh, lax.rem(s + 2, 64))
    lower = (zh, lax.rem(s + 62, 64))
    sibling = device(zh, x, zl, y, 1 - c)

    loads = {}
    def load(name, src, dst, i):
        loads[name] = pltpu.make_async_copy(src, dst, in_sem.at[i])
        loads[name].start()
    load("x0", x_hbm.at[0], x_v.at[0], 0)
    load("w0", w_hbm.at[0], w_v.at[0], 3)
    load("w2", w_hbm.at[2], w_v.at[2], 5)
    load("x1", x_hbm.at[1], x_v.at[1], 1)
    load("x2", x_hbm.at[2], x_v.at[2], 2)
    load("w1", w_hbm.at[1], w_v.at[1], 4)
    load("p", p_hbm, p_v, 6)
    load("g", g_hbm, g_v, 7)

    barrier = pltpu.get_barrier_semaphore()
    def greet(peer):
        pl.semaphore_signal(barrier, inc=1, device_id=peer, device_id_type=MESH)
    greet(upper)
    greet(lower)
    greet(sibling)
    for k in (1, 2, 3):
        greet(device(zh, lax.rem(x + k, 4), zl, y, c))
        greet(device(zh, x, zl, lax.rem(y + k, 4), c))
    for kz in range(4):
        for kl in range(2):
            peer = device(lax.rem(zh + kz, 4), x, lax.rem(zl + c + kl, 2), y, zl)
            if kz == 0:
                is_self = jnp.logical_and(lax.rem(c + kl, 2) == 0, c == zl)
                @pl.when(jnp.logical_not(is_self))
                def _(peer=peer):
                    greet(peer)
            else:
                greet(peer)

    def send_halo(src, dst, sem, ssem, ch, w, to):
        pltpu.make_async_remote_copy(
            src_ref=src.at[ch, pl.ds(w * BINS, BINS)],
            dst_ref=dst.at[ch, pl.ds(w * BINS, BINS)],
            send_sem=ph_send_sem.at[ssem],
            recv_sem=sem.at[ch, w],
            device_id=to,
            device_id_type=MESH,
        ).start()

    def wait_halo(dst, sem, ch, w):
        ref = dst.at[ch, pl.ds(w * BINS, BINS)]
        pltpu.make_async_remote_copy(
            src_ref=ref, dst_ref=ref, send_sem=ph_send_sem.at[0], recv_sem=sem.at[ch, w],
            device_id=upper, device_id_type=MESH,
        ).wait_recv()

    SLAB = 16
    for w in range(WIN):
        loads["x%d" % w].wait()
        def activate(i, carry, w=w):
            r = pl.multiple_of(i * SLAB, SLAB)
            v = x_v[w, pl.ds(r, SLAB), :].astype(F32)
            value, slope = gelu_parts(v)
            act[pl.ds(w * BINS + r, SLAB), :] = value.astype(BF16)
            slope_x[pl.ds(w * BINS + r, SLAB), :] = slope
            return carry
        lax.fori_loop(0, BINS // SLAB, activate, 0)
        a_w = act[pl.ds(w * BINS, BINS), :]
        if w == 0:
            loads["w0"].wait()
        u = dot(a_w, w_v[0]).astype(BF16)
        for ch in range(CHUNKS):
            u_send[ch, pl.ds(w * BINS, BINS), :] = u[:, ch * COL:(ch + 1) * COL]
        if w == 0:
            pl.semaphore_wait(barrier, 2 + 1 + 3 + 3 + 7 + off)
        send_halo(u_send, u_recv, u_sem, 0, 0, w, upper)
        if w == 0:
            loads["w2"].wait()
        v = dot(a_w, w_v[2]).astype(BF16)
        for ch in range(CHUNKS):
            v_send[ch, pl.ds(w * BINS, BINS), :] = v[:, ch * COL:(ch + 1) * COL]
        send_halo(v_send, v_recv, v_sem, 1, 0, w, lower)

    def send_products(ch):
        for w in range(WIN):
            send_halo(u_send, u_recv, u_sem, 0, ch, w, upper)
            send_halo(v_send, v_recv, v_sem, 1, ch, w, lower)

    send_products(1)

    loads["w1"].wait()
    loads["p"].wait()
    loads["g"].wait()
    for w in range(WIN):
        rows = pl.ds(w * BINS, BINS)
        cpre[rows, :] = dot(act[rows, :], w_v[1])
        dmid[rows, :] = dot(g_v[w], p_v[...], 1, 1)
        act_t[:, rows] = act[rows, :].T

    def clear_if(cond, ref, ch, w):
        @pl.when(cond)
        def _():
            ref[ch, pl.ds(w * BINS, BINS), :] = jnp.zeros((BINS, COL), BF16)

    MIDSLAB = 64
    def middle(ch):
        for w in range(WIN):
            wait_halo(u_recv, u_sem, ch, w)
            wait_halo(v_recv, v_sem, ch, w)
            clear_if(s < 2, u_recv, ch, w)
            clear_if(s >= 62, v_recv, ch, w)
            def bottleneck(i, carry, w=w):
                r = pl.multiple_of(w * BINS + i * MIDSLAB, MIDSLAB)
                rows = pl.ds(r, MIDSLAB)
                cols = pl.ds(ch * COL, COL)
                pre = cpre[rows, cols] + u_recv[ch, rows, :].astype(F32) + v_recv[ch, rows, :].astype(F32)
                value, slope = gelu_parts(pre)
                mid[rows, cols] = value.astype(BF16)
                d_send[ch, rows, :] = (dmid[rows, cols] * slope).astype(BF16)
                return carry
            lax.fori_loop(0, BINS // MIDSLAB, bottleneck, 0)
            send_halo(d_send, dlo_recv, dlo_sem, 2, ch, w, upper)
            send_halo(d_send, dup_recv, dup_sem, 3, ch, w, lower)

    def centre_tap(ch):
        total[ch, pl.ds(C, C), :] = dot(act_t[...], d_send[ch])

    def unit(rnd, zh_, x_, zl_):
        start = pl.multiple_of((zh_ * 8 + x_ * 2 + zl_) * UNIT, 8)
        return total[rnd, pl.ds(start, UNIT), :]

    def part(rnd, x_, zl_):
        return jnp.concatenate([unit(rnd, k, x_, zl_) for k in range(4)], axis=0)

    def pair_copy(rnd):
        return pltpu.make_async_remote_copy(
            src_ref=pair_send.at[rnd], dst_ref=pair_recv.at[rnd],
            send_sem=pair_ssem.at[rnd], recv_sem=pair_rsem.at[rnd],
            device_id=sibling, device_id_type=MESH,
        )

    def stage_a(rnd):
        for xa in range(4):
            pair_send[rnd, pl.ds(xa * PART, PART), :] = part(rnd, xa, 1 - c).astype(BF16)
        pair_copy(rnd).start()

    def x_copy(rnd, k):
        return pltpu.make_async_remote_copy(
            src_ref=x_send.at[rnd, k - 1], dst_ref=x_recv.at[rnd, k - 1],
            send_sem=x_ssem.at[rnd, k - 1], recv_sem=x_rsem.at[rnd, k - 1],
            device_id=device(zh, lax.rem(x + k, 4), zl, y, c), device_id_type=MESH,
        )

    def both_cores(rnd, xa):
        other = pair_recv[rnd, pl.ds(pl.multiple_of(xa * PART, 16), PART), :]
        return part(rnd, xa, c) + other.astype(F32)

    step = jnp.where(zl == 1, 1, 3)

    def ring_copy(rnd, t):
        return pltpu.make_async_remote_copy(
            src_ref=x_send.at[rnd, t], dst_ref=x_recv.at[rnd, t],
            send_sem=x_ssem.at[rnd, t], recv_sem=x_rsem.at[rnd, t],
            device_id=device(zh, lax.rem(x + step, 4), zl, y, c), device_id_type=MESH,
        )

    def ring(rnd, t):
        if t == 0:
            pair_copy(rnd).wait_recv()
            part_sum = both_cores(rnd, lax.rem(x + 4 - step, 4))
        else:
            ring_copy(rnd, t - 1).wait_recv()
            xa = lax.rem(x + 2, 4) if t == 1 else lax.rem(x + step, 4)
            part_sum = both_cores(rnd, xa) + x_recv[rnd, t - 1].astype(F32)
        x_send[rnd, t] = part_sum.astype(BF16)
        ring_copy(rnd, t).start()

    def straight(rnd):
        pair_copy(rnd).wait_recv()
        for k in (2, 1, 3):
            x_send[rnd, k - 1] = both_cores(rnd, lax.rem(x + k, 4)).astype(BF16)
            x_copy(rnd, k).start()

    def y_copy(rnd, k):
        return pltpu.make_async_remote_copy(
            src_ref=y_send.at[rnd, k - 1], dst_ref=y_recv.at[rnd, k - 1],
            send_sem=y_ssem.at[rnd, k - 1], recv_sem=y_rsem.at[rnd, k - 1],
            device_id=device(zh, x, zl, lax.rem(y + k, 4), c), device_id_type=MESH,
        )

    def along_y(rnd):
        mine = both_cores(rnd, x)
        if rnd == LAST:
            for k in (1, 3, 2):
                x_copy(rnd, k).wait_recv()
            mine = mine + x_recv[rnd, 0].astype(F32) + x_recv[rnd, 1].astype(F32)
        else:
            ring_copy(rnd, 2).wait_recv()
        acc[rnd] = mine + x_recv[rnd, 2].astype(F32)
        for ya in range(4):
            for za in range(4):
                y_sum[rnd, ya, pl.ds(za * LINE, LINE), :] = acc[rnd, pl.ds(za * UNIT + ya * LINE, LINE), :]
            y_sum[rnd, ya, pl.ds(UNIT, 8), :] = jnp.zeros((8, COL), F32)
        for k in (2, 1, 3):
            y_send[rnd, k - 1] = y_sum[rnd, lax.rem(y + k, 4)].astype(BF16)
            y_copy(rnd, k).start()

    def z_copy(rnd, kz, kc):
        za = lax.rem(zh + kz, 4)
        ca = lax.rem(c + kc, 2)
        return pltpu.make_async_remote_copy(
            src_ref=z_send.at[rnd, za * 2 + ca], dst_ref=z_recv.at[rnd, kz * 2 + off],
            send_sem=z_ssem.at[rnd], recv_sem=z_rsem.at[rnd],
            device_id=device(za, x, c, y, ca), device_id_type=MESH,
        )

    def along_z(rnd):
        for k in (1, 3, 2):
            y_copy(rnd, k).wait_recv()
        z_sum[rnd] = (
            y_sum[rnd, y] + y_recv[rnd, 0].astype(F32)
            + y_recv[rnd, 1].astype(F32) + y_recv[rnd, 2].astype(F32)
        )
        for b in range(8):
            z_send[rnd, b] = z_sum[rnd, pl.ds(OWN * b, 16), :].astype(BF16)
        for kz in (2, 1, 3, 0):
            for kc in (1, 0):
                if kz == 0 and kc == 0:
                    @pl.when(off == 0)
                    def _():
                        z_recv[rnd, 0] = z_send[rnd, zh * 2 + c]
                    @pl.when(off == 1)
                    def _():
                        z_copy(rnd, 0, 0).start()
                else:
                    z_copy(rnd, kz, kc).start()

    def z_wait(rnd, recv):
        def wait(first):
            copy = pltpu.make_async_remote_copy(
                src_ref=z_send.at[rnd, pl.ds(first, 8 - first)],
                dst_ref=z_recv.at[rnd, pl.ds(first, 8 - first)],
                send_sem=z_ssem.at[rnd], recv_sem=z_rsem.at[rnd],
                device_id=sibling, device_id_type=MESH,
            )
            if recv:
                copy.wait_recv()
            else:
                copy.wait_send()
        @pl.when(off == 0)
        def _():
            wait(1)
        @pl.when(off == 1)
        def _():
            wait(0)

    def finish(rnd):
        z_wait(rnd, True)
        result = jnp.sum(z_recv[rnd].astype(F32), axis=0)[:OWN] * factor
        if rnd == PROJ:
            proj_ref[...] = result
        else:
            conv_ref[pl.ds(rnd, OWN, stride=CHUNKS), :] = result

    def projection():
        grad = dot(mid[pl.ds(0, BINS), :], g_v[0], 0, 0)
        for w in range(1, WIN):
            grad = grad + dot(mid[pl.ds(w * BINS, BINS), :], g_v[w], 0, 0)
        for j in range(C // COL):
            total[PROJ, pl.ds(j, BN, stride=C // COL), :] = grad[:, j * COL:(j + 1) * COL]

    stores = []
    def store(src, dst):
        copy = pltpu.make_async_copy(src, dst, out_sem.at[len(stores)])
        copy.start()
        stores.append(copy)

    def block_output():
        for w in range(WIN):
            rows = pl.ds(w * BINS, BINS)
            out_v[w] = (x_v[w].astype(F32) + dot(mid[rows, :], p_v[...])).astype(BF16)
        store(out_v, out_hbm)

    def outer_taps(ch):
        for w in range(WIN):
            wait_halo(dup_recv, dup_sem, ch, w)
            wait_halo(dlo_recv, dlo_sem, ch, w)
            clear_if(s < 2, dlo_recv, ch, w)
            clear_if(s >= 62, dup_recv, ch, w)
        total[ch, pl.ds(0, C), :] = dot(act_t[...], dup_recv[ch])
        total[ch, pl.ds(2 * C, C), :] = dot(act_t[...], dlo_recv[ch])

    def input_side(ch):
        cols = pl.ds(ch * COL, COL)
        for w in range(WIN):
            rows = pl.ds(w * BINS, BINS)
            term = (
                dot(dup_recv[ch, rows, :], w_v[0, :, cols], 1, 1)
                + dot(d_send[ch, rows, :], w_v[1, :, cols], 1, 1)
                + dot(dlo_recv[ch, rows, :], w_v[2, :, cols], 1, 1)
            )
            if ch:
                term = term + dact[rows, :]
            if ch < CHUNKS - 1:
                dact[rows, :] = term
            else:
                dx_v[w] = (g_v[w].astype(F32) + term * slope_x[rows, :]).astype(BF16)

    middle(0)
    send_products(2)
    centre_tap(0)
    middle(1)
    centre_tap(1)
    outer_taps(0)
    stage_a(0)
    input_side(0)
    ring(0, 0)
    middle(2)
    centre_tap(2)
    ring(0, 1)
    projection()
    stage_a(PROJ)
    block_output()
    ring(PROJ, 0)
    ring(0, 2)
    outer_taps(1)
    stage_a(1)
    ring(PROJ, 1)
    input_side(1)
    ring(1, 0)
    ring(PROJ, 2)
    outer_taps(2)
    stage_a(2)
    ring(1, 1)
    along_y(0)
    along_y(PROJ)
    straight(2)
    ring(1, 2)
    input_side(2)
    store(dx_v, dx_hbm)
    along_z(0)
    along_z(PROJ)
    along_y(1)
    along_y(2)
    along_z(1)
    finish(0)
    finish(PROJ)
    along_z(2)
    finish(1)

    for i, (ref, to) in enumerate(((u_send, upper), (v_send, lower), (d_send, upper), (d_send, lower))):
        pltpu.make_async_remote_copy(
            src_ref=ref, dst_ref=ref, send_sem=ph_send_sem.at[i], recv_sem=u_sem.at[0, 0],
            device_id=to, device_id_type=MESH,
        ).wait_send()
    for rnd in range(ROUNDS):
        pair_copy(rnd).wait_send()
        for k in (1, 2, 3):
            x_copy(rnd, k).wait_send()
            y_copy(rnd, k).wait_send()
        z_wait(rnd, False)
    finish(LAST)
    for copy in stores:
        copy.wait()


def local(inputs, dilated_tap_weight, proj_weight, cotangent):
    total_rows = inputs.shape[0] * lax.axis_size("dp") * inputs.shape[1] * lax.axis_size("seq")
    factor = 1.0 / math.sqrt(total_rows)
    vm = pltpu.VMEM
    dma = pltpu.SemaphoreType.DMA
    halo = (CHUNKS, ROWS, COL)
    hbm = pl.BlockSpec(memory_space=pl.ANY)
    vmem = pl.BlockSpec(memory_space=pltpu.VMEM)
    return pl.pallas_call(
        functools.partial(kernel, factor),
        out_shape=(
            jax.ShapeDtypeStruct(inputs.shape, BF16),
            jax.ShapeDtypeStruct(inputs.shape, BF16),
            jax.ShapeDtypeStruct((CHUNKS * OWN, COL), F32),
            jax.ShapeDtypeStruct((OWN, COL), F32),
        ),
        in_specs=[hbm] * 4,
        out_specs=(hbm, hbm, vmem, vmem),
        scratch_shapes=[
            vm((WIN, BINS, C), BF16), vm((3, C, BN), BF16), vm((BN, C), BF16), vm((WIN, BINS, C), BF16),
            vm((ROWS, C), BF16), vm((C, ROWS), BF16), vm((ROWS, C), F32),
            vm((ROWS, BN), F32), vm((ROWS, BN), F32), vm((ROWS, BN), BF16), vm((ROWS, C), F32),
            vm((WIN, BINS, C), BF16), vm((WIN, BINS, C), BF16),
            vm(halo, BF16), vm(halo, BF16), vm(halo, BF16), vm(halo, BF16),
            vm(halo, BF16), vm(halo, BF16), vm(halo, BF16),
            vm((ROUNDS, ALL, COL), F32),
            vm((ROUNDS, 4 * PART, COL), BF16), vm((ROUNDS, 4 * PART, COL), BF16),
            vm((ROUNDS, 3, PART, COL), BF16), vm((ROUNDS, 3, PART, COL), BF16),
            vm((ROUNDS, PART, COL), F32),
            vm((ROUNDS, 4, UNIT + 8, COL), F32),
            vm((ROUNDS, 3, UNIT + 8, COL), BF16), vm((ROUNDS, 3, UNIT + 8, COL), BF16),
            vm((ROUNDS, UNIT + 8, COL), F32),
            vm((ROUNDS, 8, 16, COL), BF16), vm((ROUNDS, 8, 16, COL), BF16),
            dma((8,)), dma((2,)), dma((4,)),
            dma((CHUNKS, WIN)), dma((CHUNKS, WIN)), dma((CHUNKS, WIN)), dma((CHUNKS, WIN)),
            dma((ROUNDS,)), dma((ROUNDS,)), dma((ROUNDS, 3)), dma((ROUNDS, 3)),
            dma((ROUNDS, 3)), dma((ROUNDS, 3)),
            dma((ROUNDS,)), dma((ROUNDS,)),
        ],
        compiler_params=pltpu.CompilerParams(
            collective_id=0, has_side_effects=True, vmem_limit_bytes=56 * 1024 * 1024
        ),
        name="block",
    )(inputs, dilated_tap_weight, proj_weight, cotangent)


def solution(mesh):
    return jax.shard_map(
        local,
        mesh=mesh,
        in_specs=(P("dp", "seq", None), P(), P(), P("dp", "seq", None)),
        out_specs=(
            P("dp", "seq", None),
            P("dp", "seq", None),
            P(("dp", "seq"), None),
            P(("dp", "seq"), None),
        ),
        check_vma=False,
    )
```

```python
import functools
import math

import jax
import jax.numpy as jnp
from jax import lax
from jax.experimental import pallas as pl
from jax.experimental.pallas import tpu as pltpu
from jax.sharding import PartitionSpec as P

MESH = pl.DeviceIdType.MESH
F32 = jnp.float32
BF16 = jnp.bfloat16
SLOPE = math.sqrt(2.0 / math.pi)
CUBIC = 0.044715

WIN = 3
BINS = 256
ROWS = WIN * BINS
C = 768
BN = 384
COL = 128
CHUNKS = BN // COL
PROJ = CHUNKS
ROUNDS = CHUNKS + 1
LAST = CHUNKS - 1
ALL = 2304
UNIT = 72
PART = 4 * UNIT
LINE = 18
OWN = 9


def gelu_parts(v):
    sq = v * v
    t = jnp.tanh(SLOPE * v * (1.0 + CUBIC * sq))
    half = 0.5 * (1.0 + t)
    value = v * half
    slope = half + (0.5 * SLOPE) * v * (1.0 - t * t) * (1.0 + (3.0 * CUBIC) * sq)
    return value, slope


def dot(a, b, ca=1, cb=0):
    return lax.dot_general(a, b, (((ca,), (cb,)), ((), ())), preferred_element_type=F32)


def kernel(
    factor,
    x_hbm, w_hbm, p_hbm, g_hbm,
    out_v, dx_v, conv_ref, proj_ref,
    x_v, w_v, p_v, g_v, act, act_t, slope_x, cpre, dmid, mid, dact,
    u_send, v_send, u_recv, v_recv, d_send, dup_recv, dlo_recv,
    total, pair_send, pair_recv, x_send, x_recv, acc,
    y_sum, y_send, y_recv, z_sum, z_send, z_recv,
    in_sem, ph_send_sem, u_sem, v_sem, dup_sem, dlo_sem,
    pair_ssem, pair_rsem, x_ssem, x_rsem, y_ssem, y_rsem, z_ssem, z_rsem,
):
    zh = lax.axis_index("dp")
    s = lax.axis_index("seq")
    x = s // 16
    zl = lax.rem(s // 8, 2)
    y = lax.rem(s // 2, 4)
    c = lax.rem(s, 2)
    off = lax.rem(zl + c, 2)

    def device(zh_, x_, zl_, y_, c_):
        return (zh_, ((x_ * 2 + zl_) * 4 + y_) * 2 + c_)

    upper = (zh, lax.rem(s + 2, 64))
    lower = (zh, lax.rem(s + 62, 64))
    sibling = device(zh, x, zl, y, 1 - c)

    loads = {}
    def load(name, src, dst, i):
        loads[name] = pltpu.make_async_copy(src, dst, in_sem.at[i])
        loads[name].start()
    load("x0", x_hbm.at[0], x_v.at[0], 0)
    load("w0", w_hbm.at[0], w_v.at[0], 3)
    load("w2", w_hbm.at[2], w_v.at[2], 5)
    load("x1", x_hbm.at[1], x_v.at[1], 1)
    load("x2", x_hbm.at[2], x_v.at[2], 2)
    load("w1", w_hbm.at[1], w_v.at[1], 4)
    load("p", p_hbm, p_v, 6)
    load("g", g_hbm, g_v, 7)

    barrier = pltpu.get_barrier_semaphore()
    def greet(peer):
        pl.semaphore_signal(barrier, inc=1, device_id=peer, device_id_type=MESH)
    greet(upper)
    greet(lower)
    greet(sibling)
    for k in (1, 2, 3):
        greet(device(zh, lax.rem(x + k, 4), zl, y, c))
        greet(device(zh, x, zl, lax.rem(y + k, 4), c))
    for kz in range(4):
        for kl in range(2):
            peer = device(lax.rem(zh + kz, 4), x, lax.rem(zl + c + kl, 2), y, zl)
            if kz == 0:
                is_self = jnp.logical_and(lax.rem(c + kl, 2) == 0, c == zl)
                @pl.when(jnp.logical_not(is_self))
                def _(peer=peer):
                    greet(peer)
            else:
                greet(peer)

    def send_halo(src, dst, sem, ssem, ch, w, to):
        pltpu.make_async_remote_copy(
            src_ref=src.at[ch, pl.ds(w * BINS, BINS)],
            dst_ref=dst.at[ch, pl.ds(w * BINS, BINS)],
            send_sem=ph_send_sem.at[ssem],
            recv_sem=sem.at[ch, w],
            device_id=to,
            device_id_type=MESH,
        ).start()

    def wait_halo(dst, sem, ch, w):
        ref = dst.at[ch, pl.ds(w * BINS, BINS)]
        pltpu.make_async_remote_copy(
            src_ref=ref, dst_ref=ref, send_sem=ph_send_sem.at[0], recv_sem=sem.at[ch, w],
            device_id=upper, device_id_type=MESH,
        ).wait_recv()

    SLAB = 16
    for w in range(WIN):
        loads["x%d" % w].wait()
        def activate(i, carry, w=w):
            r = pl.multiple_of(i * SLAB, SLAB)
            v = x_v[w, pl.ds(r, SLAB), :].astype(F32)
            value, slope = gelu_parts(v)
            act[pl.ds(w * BINS + r, SLAB), :] = value.astype(BF16)
            slope_x[pl.ds(w * BINS + r, SLAB), :] = slope
            return carry
        lax.fori_loop(0, BINS // SLAB, activate, 0)
        a_w = act[pl.ds(w * BINS, BINS), :]
        if w == 0:
            loads["w0"].wait()
        u = dot(a_w, w_v[0]).astype(BF16)
        for ch in range(CHUNKS):
            u_send[ch, pl.ds(w * BINS, BINS), :] = u[:, ch * COL:(ch + 1) * COL]
        if w == 0:
            pl.semaphore_wait(barrier, 2 + 1 + 3 + 3 + 7 + off)
        send_halo(u_send, u_recv, u_sem, 0, 0, w, upper)
        if w == 0:
            loads["w2"].wait()
        v = dot(a_w, w_v[2]).astype(BF16)
        for ch in range(CHUNKS):
            v_send[ch, pl.ds(w * BINS, BINS), :] = v[:, ch * COL:(ch + 1) * COL]
        send_halo(v_send, v_recv, v_sem, 1, 0, w, lower)

    def send_products(ch):
        for w in range(WIN):
            send_halo(u_send, u_recv, u_sem, 0, ch, w, upper)
            send_halo(v_send, v_recv, v_sem, 1, ch, w, lower)

    send_products(1)

    loads["w1"].wait()
    loads["p"].wait()
    loads["g"].wait()
    for w in range(WIN):
        rows = pl.ds(w * BINS, BINS)
        cpre[rows, :] = dot(act[rows, :], w_v[1])
        dmid[rows, :] = dot(g_v[w], p_v[...], 1, 1)
        act_t[:, rows] = act[rows, :].T

    def clear_if(cond, ref, ch, w):
        @pl.when(cond)
        def _():
            ref[ch, pl.ds(w * BINS, BINS), :] = jnp.zeros((BINS, COL), BF16)

    MIDSLAB = 64
    def middle(ch):
        for w in range(WIN):
            wait_halo(u_recv, u_sem, ch, w)
            wait_halo(v_recv, v_sem, ch, w)
            clear_if(s < 2, u_recv, ch, w)
            clear_if(s >= 62, v_recv, ch, w)
            def bottleneck(i, carry, w=w):
                r = pl.multiple_of(w * BINS + i * MIDSLAB, MIDSLAB)
                rows = pl.ds(r, MIDSLAB)
                cols = pl.ds(ch * COL, COL)
                pre = cpre[rows, cols] + u_recv[ch, rows, :].astype(F32) + v_recv[ch, rows, :].astype(F32)
                value, slope = gelu_parts(pre)
                mid[rows, cols] = value.astype(BF16)
                d_send[ch, rows, :] = (dmid[rows, cols] * slope).astype(BF16)
                return carry
            lax.fori_loop(0, BINS // MIDSLAB, bottleneck, 0)
            send_halo(d_send, dlo_recv, dlo_sem, 2, ch, w, upper)
            send_halo(d_send, dup_recv, dup_sem, 3, ch, w, lower)

    def centre_tap(ch):
        total[ch, pl.ds(C, C), :] = dot(act_t[...], d_send[ch])

    def unit(rnd, zh_, x_, zl_):
        start = pl.multiple_of((zh_ * 8 + x_ * 2 + zl_) * UNIT, 8)
        return total[rnd, pl.ds(start, UNIT), :]

    def part(rnd, x_, zl_):
        return jnp.concatenate([unit(rnd, k, x_, zl_) for k in range(4)], axis=0)

    def pair_copy(rnd):
        return pltpu.make_async_remote_copy(
            src_ref=pair_send.at[rnd], dst_ref=pair_recv.at[rnd],
            send_sem=pair_ssem.at[rnd], recv_sem=pair_rsem.at[rnd],
            device_id=sibling, device_id_type=MESH,
        )

    def stage_a(rnd):
        for xa in range(4):
            pair_send[rnd, pl.ds(xa * PART, PART), :] = part(rnd, xa, 1 - c).astype(BF16)
        pair_copy(rnd).start()

    def x_copy(rnd, k):
        return pltpu.make_async_remote_copy(
            src_ref=x_send.at[rnd, k - 1], dst_ref=x_recv.at[rnd, k - 1],
            send_sem=x_ssem.at[rnd, k - 1], recv_sem=x_rsem.at[rnd, k - 1],
            device_id=device(zh, lax.rem(x + k, 4), zl, y, c), device_id_type=MESH,
        )

    def both_cores(rnd, xa):
        other = pair_recv[rnd, pl.ds(pl.multiple_of(xa * PART, 16), PART), :]
        return part(rnd, xa, c) + other.astype(F32)

    step = jnp.where(zl == 1, 1, 3)

    def ring_copy(rnd, t):
        return pltpu.make_async_remote_copy(
            src_ref=x_send.at[rnd, t], dst_ref=x_recv.at[rnd, t],
            send_sem=x_ssem.at[rnd, t], recv_sem=x_rsem.at[rnd, t],
            device_id=device(zh, lax.rem(x + step, 4), zl, y, c), device_id_type=MESH,
        )

    def ring(rnd, t):
        if t == 0:
            pair_copy(rnd).wait_recv()
            part_sum = both_cores(rnd, lax.rem(x + 4 - step, 4))
        else:
            ring_copy(rnd, t - 1).wait_recv()
            xa = lax.rem(x + 2, 4) if t == 1 else lax.rem(x + step, 4)
            part_sum = both_cores(rnd, xa) + x_recv[rnd, t - 1].astype(F32)
        x_send[rnd, t] = part_sum.astype(BF16)
        ring_copy(rnd, t).start()

    def straight(rnd):
        pair_copy(rnd).wait_recv()
        for k in (2, 1, 3):
            x_send[rnd, k - 1] = both_cores(rnd, lax.rem(x + k, 4)).astype(BF16)
            x_copy(rnd, k).start()

    def y_copy(rnd, k):
        return pltpu.make_async_remote_copy(
            src_ref=y_send.at[rnd, k - 1], dst_ref=y_recv.at[rnd, k - 1],
            send_sem=y_ssem.at[rnd, k - 1], recv_sem=y_rsem.at[rnd, k - 1],
            device_id=device(zh, x, zl, lax.rem(y + k, 4), c), device_id_type=MESH,
        )

    def along_y(rnd):
        mine = both_cores(rnd, x)
        if rnd == LAST:
            for k in (1, 3, 2):
                x_copy(rnd, k).wait_recv()
            mine = mine + x_recv[rnd, 0].astype(F32) + x_recv[rnd, 1].astype(F32)
        else:
            ring_copy(rnd, 2).wait_recv()
        acc[rnd] = mine + x_recv[rnd, 2].astype(F32)
        for ya in range(4):
            for za in range(4):
                y_sum[rnd, ya, pl.ds(za * LINE, LINE), :] = acc[rnd, pl.ds(za * UNIT + ya * LINE, LINE), :]
            y_sum[rnd, ya, pl.ds(UNIT, 8), :] = jnp.zeros((8, COL), F32)
        for k in (2, 1, 3):
            y_send[rnd, k - 1] = y_sum[rnd, lax.rem(y + k, 4)].astype(BF16)
            y_copy(rnd, k).start()

    def z_copy(rnd, kz, kc):
        za = lax.rem(zh + kz, 4)
        ca = lax.rem(c + kc, 2)
        return pltpu.make_async_remote_copy(
            src_ref=z_send.at[rnd, za * 2 + ca], dst_ref=z_recv.at[rnd, kz * 2 + off],
            send_sem=z_ssem.at[rnd], recv_sem=z_rsem.at[rnd],
            device_id=device(za, x, c, y, ca), device_id_type=MESH,
        )

    def along_z(rnd):
        for k in (1, 3, 2):
            y_copy(rnd, k).wait_recv()
        z_sum[rnd] = (
            y_sum[rnd, y] + y_recv[rnd, 0].astype(F32)
            + y_recv[rnd, 1].astype(F32) + y_recv[rnd, 2].astype(F32)
        )
        for b in range(8):
            z_send[rnd, b] = z_sum[rnd, pl.ds(OWN * b, 16), :].astype(BF16)
        for kz in (2, 1, 3, 0):
            for kc in (1, 0):
                if kz == 0 and kc == 0:
                    @pl.when(off == 0)
                    def _():
                        z_recv[rnd, 0] = z_send[rnd, zh * 2 + c]
                    @pl.when(off == 1)
                    def _():
                        z_copy(rnd, 0, 0).start()
                else:
                    z_copy(rnd, kz, kc).start()

    def z_wait(rnd, recv):
        def wait(first):
            copy = pltpu.make_async_remote_copy(
                src_ref=z_send.at[rnd, pl.ds(first, 8 - first)],
                dst_ref=z_recv.at[rnd, pl.ds(first, 8 - first)],
                send_sem=z_ssem.at[rnd], recv_sem=z_rsem.at[rnd],
                device_id=sibling, device_id_type=MESH,
            )
            if recv:
                copy.wait_recv()
            else:
                copy.wait_send()
        @pl.when(off == 0)
        def _():
            wait(1)
        @pl.when(off == 1)
        def _():
            wait(0)

    def finish(rnd):
        z_wait(rnd, True)
        result = jnp.sum(z_recv[rnd].astype(F32), axis=0)[:OWN] * factor
        if rnd == PROJ:
            proj_ref[...] = result
        else:
            conv_ref[pl.ds(rnd, OWN, stride=CHUNKS), :] = result

    def projection():
        grad = dot(mid[pl.ds(0, BINS), :], g_v[0], 0, 0)
        for w in range(1, WIN):
            grad = grad + dot(mid[pl.ds(w * BINS, BINS), :], g_v[w], 0, 0)
        for j in range(C // COL):
            total[PROJ, pl.ds(j, BN, stride=C // COL), :] = grad[:, j * COL:(j + 1) * COL]

    def block_output():
        for w in range(WIN):
            rows = pl.ds(w * BINS, BINS)
            out_v[w] = (x_v[w].astype(F32) + dot(mid[rows, :], p_v[...])).astype(BF16)

    def outer_taps(ch):
        for w in range(WIN):
            wait_halo(dup_recv, dup_sem, ch, w)
            wait_halo(dlo_recv, dlo_sem, ch, w)
            clear_if(s < 2, dlo_recv, ch, w)
            clear_if(s >= 62, dup_recv, ch, w)
        total[ch, pl.ds(0, C), :] = dot(act_t[...], dup_recv[ch])
        total[ch, pl.ds(2 * C, C), :] = dot(act_t[...], dlo_recv[ch])

    def input_side(ch):
        cols = pl.ds(ch * COL, COL)
        for w in range(WIN):
            rows = pl.ds(w * BINS, BINS)
            term = (
                dot(dup_recv[ch, rows, :], w_v[0, :, cols], 1, 1)
                + dot(d_send[ch, rows, :], w_v[1, :, cols], 1, 1)
                + dot(dlo_recv[ch, rows, :], w_v[2, :, cols], 1, 1)
            )
            if ch:
                term = term + dact[rows, :]
            if ch < CHUNKS - 1:
                dact[rows, :] = term
            else:
                dx_v[w] = (g_v[w].astype(F32) + term * slope_x[rows, :]).astype(BF16)

    middle(0)
    send_products(2)
    centre_tap(0)
    middle(1)
    centre_tap(1)
    outer_taps(0)
    stage_a(0)
    input_side(0)
    ring(0, 0)
    middle(2)
    centre_tap(2)
    ring(0, 1)
    projection()
    stage_a(PROJ)
    block_output()
    ring(PROJ, 0)
    ring(0, 2)
    outer_taps(1)
    stage_a(1)
    ring(PROJ, 1)
    input_side(1)
    ring(1, 0)
    ring(PROJ, 2)
    outer_taps(2)
    stage_a(2)
    ring(1, 1)
    along_y(0)
    along_y(PROJ)
    straight(2)
    ring(1, 2)
    input_side(2)
    along_z(0)
    along_z(PROJ)
    along_y(1)
    along_y(2)
    along_z(1)
    finish(0)
    finish(PROJ)
    along_z(2)
    finish(1)

    for i, (ref, to) in enumerate(((u_send, upper), (v_send, lower), (d_send, upper), (d_send, lower))):
        pltpu.make_async_remote_copy(
            src_ref=ref, dst_ref=ref, send_sem=ph_send_sem.at[i], recv_sem=u_sem.at[0, 0],
            device_id=to, device_id_type=MESH,
        ).wait_send()
    for rnd in range(ROUNDS):
        pair_copy(rnd).wait_send()
        for k in (1, 2, 3):
            x_copy(rnd, k).wait_send()
            y_copy(rnd, k).wait_send()
        z_wait(rnd, False)
    finish(LAST)


def write_out(*refs):
    *refs, sem = refs
    copies = [pltpu.make_async_copy(refs[i], refs[4 + i], sem.at[i]) for i in range(4)]
    for copy in copies:
        copy.start()
    for copy in copies:
        copy.wait()


def local(inputs, dilated_tap_weight, proj_weight, cotangent):
    total_rows = inputs.shape[0] * lax.axis_size("dp") * inputs.shape[1] * lax.axis_size("seq")
    factor = 1.0 / math.sqrt(total_rows)
    vm = pltpu.VMEM
    dma = pltpu.SemaphoreType.DMA
    halo = (CHUNKS, ROWS, COL)
    hbm = pl.BlockSpec(memory_space=pl.ANY)
    vmem = pl.BlockSpec(memory_space=pltpu.VMEM)
    results = pl.pallas_call(
        functools.partial(kernel, factor),
        out_shape=(
            vm(inputs.shape, BF16), vm(inputs.shape, BF16), vm((CHUNKS * OWN, COL), F32), vm((OWN, COL), F32),
        ),
        in_specs=[hbm] * 4,
        out_specs=(vmem,) * 4,
        scratch_shapes=[
            vm((WIN, BINS, C), BF16), vm((3, C, BN), BF16), vm((BN, C), BF16), vm((WIN, BINS, C), BF16),
            vm((ROWS, C), BF16), vm((C, ROWS), BF16), vm((ROWS, C), F32),
            vm((ROWS, BN), F32), vm((ROWS, BN), F32), vm((ROWS, BN), BF16), vm((ROWS, C), F32),
            vm(halo, BF16), vm(halo, BF16), vm(halo, BF16), vm(halo, BF16),
            vm(halo, BF16), vm(halo, BF16), vm(halo, BF16),
            vm((ROUNDS, ALL, COL), F32),
            vm((ROUNDS, 4 * PART, COL), BF16), vm((ROUNDS, 4 * PART, COL), BF16),
            vm((ROUNDS, 3, PART, COL), BF16), vm((ROUNDS, 3, PART, COL), BF16),
            vm((ROUNDS, PART, COL), F32),
            vm((ROUNDS, 4, UNIT + 8, COL), F32),
            vm((ROUNDS, 3, UNIT + 8, COL), BF16), vm((ROUNDS, 3, UNIT + 8, COL), BF16),
            vm((ROUNDS, UNIT + 8, COL), F32),
            vm((ROUNDS, 8, 16, COL), BF16), vm((ROUNDS, 8, 16, COL), BF16),
            dma((8,)), dma((4,)),
            dma((CHUNKS, WIN)), dma((CHUNKS, WIN)), dma((CHUNKS, WIN)), dma((CHUNKS, WIN)),
            dma((ROUNDS,)), dma((ROUNDS,)), dma((ROUNDS, 3)), dma((ROUNDS, 3)),
            dma((ROUNDS, 3)), dma((ROUNDS, 3)),
            dma((ROUNDS,)), dma((ROUNDS,)),
        ],
        compiler_params=pltpu.CompilerParams(
            collective_id=0, has_side_effects=True, vmem_limit_bytes=44 * 1024 * 1024
        ),
        name="block",
    )(*[pltpu.with_memory_space_constraint(a, pltpu.HBM)
        for a in (inputs, dilated_tap_weight, proj_weight, cotangent)])
    results = [pltpu.with_memory_space_constraint(r, pltpu.VMEM) for r in results]
    return pl.pallas_call(
        write_out,
        out_shape=tuple(jax.ShapeDtypeStruct(r.shape, r.dtype) for r in results),
        in_specs=[vmem] * 4,
        out_specs=(hbm,) * 4,
        scratch_shapes=[dma((4,))],
        name="write_out",
    )(*results)


def solution(mesh):
    return jax.shard_map(
        local,
        mesh=mesh,
        in_specs=(P("dp", "seq", None), P(), P(), P("dp", "seq", None)),
        out_specs=(
            P("dp", "seq", None),
            P("dp", "seq", None),
            P(("dp", "seq"), None),
            P(("dp", "seq"), None),
        ),
        check_vma=False,
    )
```

```python
import functools
import math

import jax
import jax.numpy as jnp
from jax import lax
from jax.experimental import pallas as pl
from jax.experimental.pallas import tpu as pltpu
from jax.sharding import PartitionSpec as P

MESH = pl.DeviceIdType.MESH
F32 = jnp.float32
BF16 = jnp.bfloat16
SLOPE = math.sqrt(2.0 / math.pi)
CUBIC = 0.044715

WIN = 3
BINS = 256
ROWS = WIN * BINS
C = 768
BN = 384
COL = 128
CHUNKS = BN // COL
PROJ = CHUNKS
ROUNDS = CHUNKS + 1
LAST = CHUNKS - 1
STRAIGHT = (LAST - 1, LAST)
ALL = 2304
UNIT = 72
PART = 4 * UNIT
LINE = 18
OWN = 9


def gelu_parts(v):
    sq = v * v
    t = jnp.tanh(SLOPE * v * (1.0 + CUBIC * sq))
    half = 0.5 * (1.0 + t)
    value = v * half
    slope = half + (0.5 * SLOPE) * v * (1.0 - t * t) * (1.0 + (3.0 * CUBIC) * sq)
    return value, slope


def dot(a, b, ca=1, cb=0):
    return lax.dot_general(a, b, (((ca,), (cb,)), ((), ())), preferred_element_type=F32)


def kernel(
    factor,
    x_hbm, w_hbm, p_hbm, g_hbm,
    out_v, dx_v, conv_ref, proj_ref,
    x_v, w_v, p_v, g_v, act, act_t, slope_x, cpre, dmid, mid, dact,
    u_send, v_send, u_recv, v_recv, d_send, dup_recv, dlo_recv,
    total, pair_send, pair_recv, x_send, x_recv, acc,
    y_sum, y_send, y_recv, z_sum, z_send, z_recv,
    in_sem, ph_send_sem, u_sem, v_sem, dup_sem, dlo_sem,
    pair_ssem, pair_rsem, x_ssem, x_rsem, y_ssem, y_rsem, z_ssem, z_rsem,
):
    zh = lax.axis_index("dp")
    s = lax.axis_index("seq")
    x = s // 16
    zl = lax.rem(s // 8, 2)
    y = lax.rem(s // 2, 4)
    c = lax.rem(s, 2)
    off = lax.rem(zl + c, 2)

    def device(zh_, x_, zl_, y_, c_):
        return (zh_, ((x_ * 2 + zl_) * 4 + y_) * 2 + c_)

    upper = (zh, lax.rem(s + 2, 64))
    lower = (zh, lax.rem(s + 62, 64))
    sibling = device(zh, x, zl, y, 1 - c)

    loads = {}
    def load(name, src, dst, i):
        loads[name] = pltpu.make_async_copy(src, dst, in_sem.at[i])
        loads[name].start()
    load("x0", x_hbm.at[0], x_v.at[0], 0)
    load("w0", w_hbm.at[0], w_v.at[0], 3)
    load("w2", w_hbm.at[2], w_v.at[2], 5)
    load("x1", x_hbm.at[1], x_v.at[1], 1)
    load("x2", x_hbm.at[2], x_v.at[2], 2)
    load("w1", w_hbm.at[1], w_v.at[1], 4)
    load("p", p_hbm, p_v, 6)
    load("g", g_hbm, g_v, 7)

    barrier = pltpu.get_barrier_semaphore()
    def greet(peer):
        pl.semaphore_signal(barrier, inc=1, device_id=peer, device_id_type=MESH)
    greet(upper)
    greet(lower)
    greet(sibling)
    for k in (1, 2, 3):
        greet(device(zh, lax.rem(x + k, 4), zl, y, c))
        greet(device(zh, x, zl, lax.rem(y + k, 4), c))
    for kz in range(4):
        for kl in range(2):
            peer = device(lax.rem(zh + kz, 4), x, lax.rem(zl + c + kl, 2), y, zl)
            if kz == 0:
                is_self = jnp.logical_and(lax.rem(c + kl, 2) == 0, c == zl)
                @pl.when(jnp.logical_not(is_self))
                def _(peer=peer):
                    greet(peer)
            else:
                greet(peer)

    def send_halo(src, dst, sem, ssem, ch, w, to):
        pltpu.make_async_remote_copy(
            src_ref=src.at[ch, pl.ds(w * BINS, BINS)],
            dst_ref=dst.at[ch, pl.ds(w * BINS, BINS)],
            send_sem=ph_send_sem.at[ssem],
            recv_sem=sem.at[ch, w],
            device_id=to,
            device_id_type=MESH,
        ).start()

    def wait_halo(dst, sem, ch, w):
        ref = dst.at[ch, pl.ds(w * BINS, BINS)]
        pltpu.make_async_remote_copy(
            src_ref=ref, dst_ref=ref, send_sem=ph_send_sem.at[0], recv_sem=sem.at[ch, w],
            device_id=upper, device_id_type=MESH,
        ).wait_recv()

    SLAB = 16
    for w in range(WIN):
        loads["x%d" % w].wait()
        def activate(i, carry, w=w):
            r = pl.multiple_of(i * SLAB, SLAB)
            v = x_v[w, pl.ds(r, SLAB), :].astype(F32)
            value, slope = gelu_parts(v)
            act[pl.ds(w * BINS + r, SLAB), :] = value.astype(BF16)
            slope_x[pl.ds(w * BINS + r, SLAB), :] = slope
            return carry
        lax.fori_loop(0, BINS // SLAB, activate, 0)
        a_w = act[pl.ds(w * BINS, BINS), :]
        if w == 0:
            loads["w0"].wait()
        u = dot(a_w, w_v[0]).astype(BF16)
        for ch in range(CHUNKS):
            u_send[ch, pl.ds(w * BINS, BINS), :] = u[:, ch * COL:(ch + 1) * COL]
        if w == 0:
            pl.semaphore_wait(barrier, 2 + 1 + 3 + 3 + 7 + off)
        send_halo(u_send, u_recv, u_sem, 0, 0, w, upper)
        if w == 0:
            loads["w2"].wait()
        v = dot(a_w, w_v[2]).astype(BF16)
        for ch in range(CHUNKS):
            v_send[ch, pl.ds(w * BINS, BINS), :] = v[:, ch * COL:(ch + 1) * COL]
        send_halo(v_send, v_recv, v_sem, 1, 0, w, lower)

    def send_products(ch):
        for w in range(WIN):
            send_halo(u_send, u_recv, u_sem, 0, ch, w, upper)
            send_halo(v_send, v_recv, v_sem, 1, ch, w, lower)

    send_products(1)

    loads["w1"].wait()
    loads["p"].wait()
    loads["g"].wait()
    for w in range(WIN):
        rows = pl.ds(w * BINS, BINS)
        cpre[rows, :] = dot(act[rows, :], w_v[1])
        dmid[rows, :] = dot(g_v[w], p_v[...], 1, 1)
        act_t[:, rows] = act[rows, :].T

    def clear_if(cond, ref, ch, w):
        @pl.when(cond)
        def _():
            ref[ch, pl.ds(w * BINS, BINS), :] = jnp.zeros((BINS, COL), BF16)

    MIDSLAB = 64
    def middle(ch):
        for w in range(WIN):
            wait_halo(u_recv, u_sem, ch, w)
            wait_halo(v_recv, v_sem, ch, w)
            clear_if(s < 2, u_recv, ch, w)
            clear_if(s >= 62, v_recv, ch, w)
            def bottleneck(i, carry, w=w):
                r = pl.multiple_of(w * BINS + i * MIDSLAB, MIDSLAB)
                rows = pl.ds(r, MIDSLAB)
                cols = pl.ds(ch * COL, COL)
                pre = cpre[rows, cols] + u_recv[ch, rows, :].astype(F32) + v_recv[ch, rows, :].astype(F32)
                value, slope = gelu_parts(pre)
                mid[rows, cols] = value.astype(BF16)
                d_send[ch, rows, :] = (dmid[rows, cols] * slope).astype(BF16)
                return carry
            lax.fori_loop(0, BINS // MIDSLAB, bottleneck, 0)
            send_halo(d_send, dlo_recv, dlo_sem, 2, ch, w, upper)
            send_halo(d_send, dup_recv, dup_sem, 3, ch, w, lower)

    def centre_tap(ch):
        total[ch, pl.ds(C, C), :] = dot(act_t[...], d_send[ch])

    def unit(rnd, zh_, x_, zl_):
        start = pl.multiple_of((zh_ * 8 + x_ * 2 + zl_) * UNIT, 8)
        return total[rnd, pl.ds(start, UNIT), :]

    def part(rnd, x_, zl_):
        return jnp.concatenate([unit(rnd, k, x_, zl_) for k in range(4)], axis=0)

    def pair_copy(rnd):
        return pltpu.make_async_remote_copy(
            src_ref=pair_send.at[rnd], dst_ref=pair_recv.at[rnd],
            send_sem=pair_ssem.at[rnd], recv_sem=pair_rsem.at[rnd],
            device_id=sibling, device_id_type=MESH,
        )

    def stage_a(rnd):
        for xa in range(4):
            pair_send[rnd, pl.ds(xa * PART, PART), :] = part(rnd, xa, 1 - c).astype(BF16)
        pair_copy(rnd).start()

    def x_copy(rnd, k):
        return pltpu.make_async_remote_copy(
            src_ref=x_send.at[rnd, k - 1], dst_ref=x_recv.at[rnd, k - 1],
            send_sem=x_ssem.at[rnd, k - 1], recv_sem=x_rsem.at[rnd, k - 1],
            device_id=device(zh, lax.rem(x + k, 4), zl, y, c), device_id_type=MESH,
        )

    def both_cores(rnd, xa):
        other = pair_recv[rnd, pl.ds(pl.multiple_of(xa * PART, 16), PART), :]
        return part(rnd, xa, c) + other.astype(F32)

    step = jnp.where(zl == 1, 1, 3)

    def ring_copy(rnd, t):
        return pltpu.make_async_remote_copy(
            src_ref=x_send.at[rnd, t], dst_ref=x_recv.at[rnd, t],
            send_sem=x_ssem.at[rnd, t], recv_sem=x_rsem.at[rnd, t],
            device_id=device(zh, lax.rem(x + step, 4), zl, y, c), device_id_type=MESH,
        )

    def ring(rnd, t):
        if t == 0:
            pair_copy(rnd).wait_recv()
            part_sum = both_cores(rnd, lax.rem(x + 4 - step, 4))
        else:
            ring_copy(rnd, t - 1).wait_recv()
            xa = lax.rem(x + 2, 4) if t == 1 else lax.rem(x + step, 4)
            part_sum = both_cores(rnd, xa) + x_recv[rnd, t - 1].astype(F32)
        x_send[rnd, t] = part_sum.astype(BF16)
        ring_copy(rnd, t).start()

    def straight(rnd):
        pair_copy(rnd).wait_recv()
        for k in (2, 1, 3):
            x_send[rnd, k - 1] = both_cores(rnd, lax.rem(x + k, 4)).astype(BF16)
            x_copy(rnd, k).start()

    def y_copy(rnd, k):
        return pltpu.make_async_remote_copy(
            src_ref=y_send.at[rnd, k - 1], dst_ref=y_recv.at[rnd, k - 1],
            send_sem=y_ssem.at[rnd, k - 1], recv_sem=y_rsem.at[rnd, k - 1],
            device_id=device(zh, x, zl, lax.rem(y + k, 4), c), device_id_type=MESH,
        )

    def along_y(rnd):
        mine = both_cores(rnd, x)
        if rnd in STRAIGHT:
            for k in (1, 3, 2):
                x_copy(rnd, k).wait_recv()
            mine = mine + x_recv[rnd, 0].astype(F32) + x_recv[rnd, 1].astype(F32)
        else:
            ring_copy(rnd, 2).wait_recv()
        acc[rnd] = mine + x_recv[rnd, 2].astype(F32)
        for ya in range(4):
            for za in range(4):
                y_sum[rnd, ya, pl.ds(za * LINE, LINE), :] = acc[rnd, pl.ds(za * UNIT + ya * LINE, LINE), :]
            y_sum[rnd, ya, pl.ds(UNIT, 8), :] = jnp.zeros((8, COL), F32)
        for k in (2, 1, 3):
            y_send[rnd, k - 1] = y_sum[rnd, lax.rem(y + k, 4)].astype(BF16)
            y_copy(rnd, k).start()

    def z_copy(rnd, kz, kc):
        za = lax.rem(zh + kz, 4)
        ca = lax.rem(c + kc, 2)
        return pltpu.make_async_remote_copy(
            src_ref=z_send.at[rnd, za * 2 + ca], dst_ref=z_recv.at[rnd, kz * 2 + off],
            send_sem=z_ssem.at[rnd], recv_sem=z_rsem.at[rnd],
            device_id=device(za, x, c, y, ca), device_id_type=MESH,
        )

    def along_z(rnd):
        for k in (1, 3, 2):
            y_copy(rnd, k).wait_recv()
        z_sum[rnd] = (
            y_sum[rnd, y] + y_recv[rnd, 0].astype(F32)
            + y_recv[rnd, 1].astype(F32) + y_recv[rnd, 2].astype(F32)
        )
        for b in range(8):
            z_send[rnd, b] = z_sum[rnd, pl.ds(OWN * b, 16), :].astype(BF16)
        for kz in (2, 1, 3, 0):
            for kc in (1, 0):
                if kz == 0 and kc == 0:
                    @pl.when(off == 0)
                    def _():
                        z_recv[rnd, 0] = z_send[rnd, zh * 2 + c]
                    @pl.when(off == 1)
                    def _():
                        z_copy(rnd, 0, 0).start()
                else:
                    z_copy(rnd, kz, kc).start()

    def z_wait(rnd, recv):
        def wait(first):
            copy = pltpu.make_async_remote_copy(
                src_ref=z_send.at[rnd, pl.ds(first, 8 - first)],
                dst_ref=z_recv.at[rnd, pl.ds(first, 8 - first)],
                send_sem=z_ssem.at[rnd], recv_sem=z_rsem.at[rnd],
                device_id=sibling, device_id_type=MESH,
            )
            if recv:
                copy.wait_recv()
            else:
                copy.wait_send()
        @pl.when(off == 0)
        def _():
            wait(1)
        @pl.when(off == 1)
        def _():
            wait(0)

    def finish(rnd):
        z_wait(rnd, True)
        result = jnp.sum(z_recv[rnd].astype(F32), axis=0)[:OWN] * factor
        if rnd == PROJ:
            proj_ref[...] = result
        else:
            conv_ref[pl.ds(rnd, OWN, stride=CHUNKS), :] = result

    def projection():
        grad = dot(mid[pl.ds(0, BINS), :], g_v[0], 0, 0)
        for w in range(1, WIN):
            grad = grad + dot(mid[pl.ds(w * BINS, BINS), :], g_v[w], 0, 0)
        for j in range(C // COL):
            total[PROJ, pl.ds(j, BN, stride=C // COL), :] = grad[:, j * COL:(j + 1) * COL]

    def block_output():
        for w in range(WIN):
            rows = pl.ds(w * BINS, BINS)
            out_v[w] = (x_v[w].astype(F32) + dot(mid[rows, :], p_v[...])).astype(BF16)

    def outer_taps(ch):
        for w in range(WIN):
            wait_halo(dup_recv, dup_sem, ch, w)
            wait_halo(dlo_recv, dlo_sem, ch, w)
            clear_if(s < 2, dlo_recv, ch, w)
            clear_if(s >= 62, dup_recv, ch, w)
        total[ch, pl.ds(0, C), :] = dot(act_t[...], dup_recv[ch])
        total[ch, pl.ds(2 * C, C), :] = dot(act_t[...], dlo_recv[ch])

    def input_side(ch):
        cols = pl.ds(ch * COL, COL)
        for w in range(WIN):
            rows = pl.ds(w * BINS, BINS)
            term = (
                dot(dup_recv[ch, rows, :], w_v[0, :, cols], 1, 1)
                + dot(d_send[ch, rows, :], w_v[1, :, cols], 1, 1)
                + dot(dlo_recv[ch, rows, :], w_v[2, :, cols], 1, 1)
            )
            if ch:
                term = term + dact[rows, :]
            if ch < CHUNKS - 1:
                dact[rows, :] = term
            else:
                dx_v[w] = (g_v[w].astype(F32) + term * slope_x[rows, :]).astype(BF16)

    middle(0)
    send_products(2)
    centre_tap(0)
    middle(1)
    centre_tap(1)
    outer_taps(0)
    stage_a(0)
    input_side(0)
    ring(0, 0)
    middle(2)
    centre_tap(2)
    ring(0, 1)
    projection()
    stage_a(PROJ)
    block_output()
    ring(PROJ, 0)
    ring(0, 2)
    outer_taps(1)
    stage_a(1)
    ring(PROJ, 1)
    input_side(1)
    straight(1)
    ring(PROJ, 2)
    outer_taps(2)
    stage_a(2)
    straight(2)
    along_y(0)
    along_y(PROJ)
    along_y(1)
    input_side(2)
    along_z(0)
    along_y(2)
    along_z(PROJ)
    along_z(1)
    along_z(2)
    finish(0)
    finish(PROJ)
    finish(1)

    for i, (ref, to) in enumerate(((u_send, upper), (v_send, lower), (d_send, upper), (d_send, lower))):
        pltpu.make_async_remote_copy(
            src_ref=ref, dst_ref=ref, send_sem=ph_send_sem.at[i], recv_sem=u_sem.at[0, 0],
            device_id=to, device_id_type=MESH,
        ).wait_send()
    for rnd in range(ROUNDS):
        pair_copy(rnd).wait_send()
        for k in (1, 2, 3):
            x_copy(rnd, k).wait_send()
            y_copy(rnd, k).wait_send()
        z_wait(rnd, False)
    finish(LAST)


def write_out(*refs):
    *refs, sem = refs
    copies = [pltpu.make_async_copy(refs[i], refs[4 + i], sem.at[i]) for i in range(4)]
    for copy in copies:
        copy.start()
    for copy in copies:
        copy.wait()


def local(inputs, dilated_tap_weight, proj_weight, cotangent):
    total_rows = inputs.shape[0] * lax.axis_size("dp") * inputs.shape[1] * lax.axis_size("seq")
    factor = 1.0 / math.sqrt(total_rows)
    vm = pltpu.VMEM
    dma = pltpu.SemaphoreType.DMA
    halo = (CHUNKS, ROWS, COL)
    hbm = pl.BlockSpec(memory_space=pl.ANY)
    vmem = pl.BlockSpec(memory_space=pltpu.VMEM)
    results = pl.pallas_call(
        functools.partial(kernel, factor),
        out_shape=(
            vm(inputs.shape, BF16), vm(inputs.shape, BF16), vm((CHUNKS * OWN, COL), F32), vm((OWN, COL), F32),
        ),
        in_specs=[hbm] * 4,
        out_specs=(vmem,) * 4,
        scratch_shapes=[
            vm((WIN, BINS, C), BF16), vm((3, C, BN), BF16), vm((BN, C), BF16), vm((WIN, BINS, C), BF16),
            vm((ROWS, C), BF16), vm((C, ROWS), BF16), vm((ROWS, C), F32),
            vm((ROWS, BN), F32), vm((ROWS, BN), F32), vm((ROWS, BN), BF16), vm((ROWS, C), F32),
            vm(halo, BF16), vm(halo, BF16), vm(halo, BF16), vm(halo, BF16),
            vm(halo, BF16), vm(halo, BF16), vm(halo, BF16),
            vm((ROUNDS, ALL, COL), F32),
            vm((ROUNDS, 4 * PART, COL), BF16), vm((ROUNDS, 4 * PART, COL), BF16),
            vm((ROUNDS, 3, PART, COL), BF16), vm((ROUNDS, 3, PART, COL), BF16),
            vm((ROUNDS, PART, COL), F32),
            vm((ROUNDS, 4, UNIT + 8, COL), F32),
            vm((ROUNDS, 3, UNIT + 8, COL), BF16), vm((ROUNDS, 3, UNIT + 8, COL), BF16),
            vm((ROUNDS, UNIT + 8, COL), F32),
            vm((ROUNDS, 8, 16, COL), BF16), vm((ROUNDS, 8, 16, COL), BF16),
            dma((8,)), dma((4,)),
            dma((CHUNKS, WIN)), dma((CHUNKS, WIN)), dma((CHUNKS, WIN)), dma((CHUNKS, WIN)),
            dma((ROUNDS,)), dma((ROUNDS,)), dma((ROUNDS, 3)), dma((ROUNDS, 3)),
            dma((ROUNDS, 3)), dma((ROUNDS, 3)),
            dma((ROUNDS,)), dma((ROUNDS,)),
        ],
        compiler_params=pltpu.CompilerParams(
            collective_id=0, has_side_effects=True, vmem_limit_bytes=44 * 1024 * 1024
        ),
        name="block",
    )(*[pltpu.with_memory_space_constraint(a, pltpu.HBM)
        for a in (inputs, dilated_tap_weight, proj_weight, cotangent)])
    results = [pltpu.with_memory_space_constraint(r, pltpu.VMEM) for r in results]
    return pl.pallas_call(
        write_out,
        out_shape=tuple(jax.ShapeDtypeStruct(r.shape, r.dtype) for r in results),
        in_specs=[vmem] * 4,
        out_specs=(hbm,) * 4,
        scratch_shapes=[dma((4,))],
        name="write_out",
    )(*results)


def solution(mesh):
    return jax.shard_map(
        local,
        mesh=mesh,
        in_specs=(P("dp", "seq", None), P(), P(), P("dp", "seq", None)),
        out_specs=(
            P("dp", "seq", None),
            P("dp", "seq", None),
            P(("dp", "seq"), None),
            P(("dp", "seq"), None),
        ),
        check_vma=False,
    )
```

```python
import functools
import math

import jax
import jax.numpy as jnp
from jax import lax
from jax.experimental import pallas as pl
from jax.experimental.pallas import tpu as pltpu
from jax.sharding import PartitionSpec as P

MESH = pl.DeviceIdType.MESH
F32 = jnp.float32
BF16 = jnp.bfloat16
SLOPE = math.sqrt(2.0 / math.pi)
CUBIC = 0.044715

WIN = 3
BINS = 256
ROWS = WIN * BINS
C = 768
BN = 384
COL = 128
CHUNKS = BN // COL
PROJ = CHUNKS
ROUNDS = CHUNKS + 1
LAST = CHUNKS - 1
STRAIGHT = (LAST - 1,)
ALL = 2304
UNIT = 72
PART = 4 * UNIT
LINE = 18
OWN = 9


def gelu_parts(v):
    sq = v * v
    t = jnp.tanh(SLOPE * v * (1.0 + CUBIC * sq))
    half = 0.5 * (1.0 + t)
    value = v * half
    slope = half + (0.5 * SLOPE) * v * (1.0 - t * t) * (1.0 + (3.0 * CUBIC) * sq)
    return value, slope


def dot(a, b, ca=1, cb=0):
    return lax.dot_general(a, b, (((ca,), (cb,)), ((), ())), preferred_element_type=F32)


def kernel(
    factor,
    x_hbm, w_hbm, p_hbm, g_hbm,
    out_v, dx_v, conv_ref, proj_ref,
    x_v, w_v, p_v, g_v, act, act_t, slope_x, cpre, dmid, mid, dact,
    u_send, v_send, u_recv, v_recv, d_send, dup_recv, dlo_recv,
    total, pair_send, pair_recv, x_send, x_recv, acc,
    y_sum, y_send, y_recv, z_sum, z_send, z_recv,
    p_acc, p_sum, p_send, p_recv,
    in_sem, ph_send_sem, u_sem, v_sem, dup_sem, dlo_sem,
    pair_ssem, pair_rsem, x_ssem, x_rsem, y_ssem, y_rsem, z_ssem, z_rsem, p_sem,
):
    zh = lax.axis_index("dp")
    s = lax.axis_index("seq")
    x = s // 16
    zl = lax.rem(s // 8, 2)
    y = lax.rem(s // 2, 4)
    c = lax.rem(s, 2)
    off = lax.rem(zl + c, 2)

    def device(zh_, x_, zl_, y_, c_):
        return (zh_, ((x_ * 2 + zl_) * 4 + y_) * 2 + c_)

    upper = (zh, lax.rem(s + 2, 64))
    lower = (zh, lax.rem(s + 62, 64))
    sibling = device(zh, x, zl, y, 1 - c)

    loads = {}
    def load(name, src, dst, i):
        loads[name] = pltpu.make_async_copy(src, dst, in_sem.at[i])
        loads[name].start()
    load("x0", x_hbm.at[0], x_v.at[0], 0)
    load("w0", w_hbm.at[0], w_v.at[0], 3)
    load("w2", w_hbm.at[2], w_v.at[2], 5)
    load("x1", x_hbm.at[1], x_v.at[1], 1)
    load("x2", x_hbm.at[2], x_v.at[2], 2)
    load("w1", w_hbm.at[1], w_v.at[1], 4)
    load("p", p_hbm, p_v, 6)
    load("g", g_hbm, g_v, 7)

    barrier = pltpu.get_barrier_semaphore()
    def greet(peer):
        pl.semaphore_signal(barrier, inc=1, device_id=peer, device_id_type=MESH)
    greet(upper)
    greet(lower)
    greet(sibling)
    for k in (1, 2, 3):
        greet(device(zh, lax.rem(x + k, 4), zl, y, c))
        greet(device(zh, x, zl, lax.rem(y + k, 4), c))
        for j in (1, 2, 3):
            greet(device(zh, lax.rem(x + k, 4), zl, lax.rem(y + j, 4), c))
    for kz in range(4):
        for kl in range(2):
            peer = device(lax.rem(zh + kz, 4), x, lax.rem(zl + c + kl, 2), y, zl)
            if kz == 0:
                is_self = jnp.logical_and(lax.rem(c + kl, 2) == 0, c == zl)
                @pl.when(jnp.logical_not(is_self))
                def _(peer=peer):
                    greet(peer)
            else:
                greet(peer)

    def send_halo(src, dst, sem, ssem, ch, w, to):
        pltpu.make_async_remote_copy(
            src_ref=src.at[ch, pl.ds(w * BINS, BINS)],
            dst_ref=dst.at[ch, pl.ds(w * BINS, BINS)],
            send_sem=ph_send_sem.at[ssem],
            recv_sem=sem.at[ch, w],
            device_id=to,
            device_id_type=MESH,
        ).start()

    def wait_halo(dst, sem, ch, w):
        ref = dst.at[ch, pl.ds(w * BINS, BINS)]
        pltpu.make_async_remote_copy(
            src_ref=ref, dst_ref=ref, send_sem=ph_send_sem.at[0], recv_sem=sem.at[ch, w],
            device_id=upper, device_id_type=MESH,
        ).wait_recv()

    SLAB = 16
    for w in range(WIN):
        loads["x%d" % w].wait()
        def activate(i, carry, w=w):
            r = pl.multiple_of(i * SLAB, SLAB)
            v = x_v[w, pl.ds(r, SLAB), :].astype(F32)
            value, slope = gelu_parts(v)
            act[pl.ds(w * BINS + r, SLAB), :] = value.astype(BF16)
            slope_x[pl.ds(w * BINS + r, SLAB), :] = slope
            return carry
        lax.fori_loop(0, BINS // SLAB, activate, 0)
        a_w = act[pl.ds(w * BINS, BINS), :]
        if w == 0:
            loads["w0"].wait()
        u = dot(a_w, w_v[0]).astype(BF16)
        for ch in range(CHUNKS):
            u_send[ch, pl.ds(w * BINS, BINS), :] = u[:, ch * COL:(ch + 1) * COL]
        if w == 0:
            pl.semaphore_wait(barrier, 2 + 1 + 15 + 7 + off)
        send_halo(u_send, u_recv, u_sem, 0, 0, w, upper)
        if w == 0:
            loads["w2"].wait()
        v = dot(a_w, w_v[2]).astype(BF16)
        for ch in range(CHUNKS):
            v_send[ch, pl.ds(w * BINS, BINS), :] = v[:, ch * COL:(ch + 1) * COL]
        send_halo(v_send, v_recv, v_sem, 1, 0, w, lower)

    def send_products(ch):
        for w in range(WIN):
            send_halo(u_send, u_recv, u_sem, 0, ch, w, upper)
            send_halo(v_send, v_recv, v_sem, 1, ch, w, lower)

    send_products(1)

    loads["w1"].wait()
    loads["p"].wait()
    loads["g"].wait()
    for w in range(WIN):
        rows = pl.ds(w * BINS, BINS)
        cpre[rows, :] = dot(act[rows, :], w_v[1])
        dmid[rows, :] = dot(g_v[w], p_v[...], 1, 1)
        act_t[:, rows] = act[rows, :].T

    def clear_if(cond, ref, ch, w):
        @pl.when(cond)
        def _():
            ref[ch, pl.ds(w * BINS, BINS), :] = jnp.zeros((BINS, COL), BF16)

    MIDSLAB = 64
    def middle(ch):
        for w in range(WIN):
            wait_halo(u_recv, u_sem, ch, w)
            wait_halo(v_recv, v_sem, ch, w)
            clear_if(s < 2, u_recv, ch, w)
            clear_if(s >= 62, v_recv, ch, w)
            def bottleneck(i, carry, w=w):
                r = pl.multiple_of(w * BINS + i * MIDSLAB, MIDSLAB)
                rows = pl.ds(r, MIDSLAB)
                cols = pl.ds(ch * COL, COL)
                pre = cpre[rows, cols] + u_recv[ch, rows, :].astype(F32) + v_recv[ch, rows, :].astype(F32)
                value, slope = gelu_parts(pre)
                mid[rows, cols] = value.astype(BF16)
                d_send[ch, rows, :] = (dmid[rows, cols] * slope).astype(BF16)
                return carry
            lax.fori_loop(0, BINS // MIDSLAB, bottleneck, 0)
            send_halo(d_send, dlo_recv, dlo_sem, 2, ch, w, upper)
            send_halo(d_send, dup_recv, dup_sem, 3, ch, w, lower)

    def centre_tap(ch):
        total[ch, pl.ds(C, C), :] = dot(act_t[...], d_send[ch])

    def unit(rnd, zh_, x_, zl_):
        start = pl.multiple_of((zh_ * 8 + x_ * 2 + zl_) * UNIT, 8)
        return total[rnd, pl.ds(start, UNIT), :]

    def part(rnd, x_, zl_):
        return jnp.concatenate([unit(rnd, k, x_, zl_) for k in range(4)], axis=0)

    def pair_copy(rnd):
        return pltpu.make_async_remote_copy(
            src_ref=pair_send.at[rnd], dst_ref=pair_recv.at[rnd],
            send_sem=pair_ssem.at[rnd], recv_sem=pair_rsem.at[rnd],
            device_id=sibling, device_id_type=MESH,
        )

    def stage_a(rnd):
        for xa in range(4):
            pair_send[rnd, pl.ds(xa * PART, PART), :] = part(rnd, xa, 1 - c).astype(BF16)
        pair_copy(rnd).start()

    def x_copy(rnd, k):
        return pltpu.make_async_remote_copy(
            src_ref=x_send.at[rnd, k - 1], dst_ref=x_recv.at[rnd, k - 1],
            send_sem=x_ssem.at[rnd, k - 1], recv_sem=x_rsem.at[rnd, k - 1],
            device_id=device(zh, lax.rem(x + k, 4), zl, y, c), device_id_type=MESH,
        )

    def both_cores(rnd, xa):
        other = pair_recv[rnd, pl.ds(pl.multiple_of(xa * PART, 16), PART), :]
        return part(rnd, xa, c) + other.astype(F32)

    step = jnp.where(zl == 1, 1, 3)

    def ring_copy(rnd, t):
        return pltpu.make_async_remote_copy(
            src_ref=x_send.at[rnd, t], dst_ref=x_recv.at[rnd, t],
            send_sem=x_ssem.at[rnd, t], recv_sem=x_rsem.at[rnd, t],
            device_id=device(zh, lax.rem(x + step, 4), zl, y, c), device_id_type=MESH,
        )

    def ring(rnd, t):
        if t == 0:
            pair_copy(rnd).wait_recv()
            part_sum = both_cores(rnd, lax.rem(x + 4 - step, 4))
        else:
            ring_copy(rnd, t - 1).wait_recv()
            xa = lax.rem(x + 2, 4) if t == 1 else lax.rem(x + step, 4)
            part_sum = both_cores(rnd, xa) + x_recv[rnd, t - 1].astype(F32)
        x_send[rnd, t] = part_sum.astype(BF16)
        ring_copy(rnd, t).start()

    def straight(rnd):
        pair_copy(rnd).wait_recv()
        for k in (2, 1, 3):
            x_send[rnd, k - 1] = both_cores(rnd, lax.rem(x + k, 4)).astype(BF16)
            x_copy(rnd, k).start()

    def y_copy(rnd, k):
        return pltpu.make_async_remote_copy(
            src_ref=y_send.at[rnd, k - 1], dst_ref=y_recv.at[rnd, k - 1],
            send_sem=y_ssem.at[rnd, k - 1], recv_sem=y_rsem.at[rnd, k - 1],
            device_id=device(zh, x, zl, lax.rem(y + k, 4), c), device_id_type=MESH,
        )

    def along_y(rnd):
        mine = both_cores(rnd, x)
        if rnd in STRAIGHT:
            for k in (1, 3, 2):
                x_copy(rnd, k).wait_recv()
            mine = mine + x_recv[rnd, 0].astype(F32) + x_recv[rnd, 1].astype(F32)
        else:
            ring_copy(rnd, 2).wait_recv()
        acc[rnd] = mine + x_recv[rnd, 2].astype(F32)
        for ya in range(4):
            for za in range(4):
                y_sum[rnd, ya, pl.ds(za * LINE, LINE), :] = acc[rnd, pl.ds(za * UNIT + ya * LINE, LINE), :]
            y_sum[rnd, ya, pl.ds(UNIT, 8), :] = jnp.zeros((8, COL), F32)
        for k in (2, 1, 3):
            y_send[rnd, k - 1] = y_sum[rnd, lax.rem(y + k, 4)].astype(BF16)
            y_copy(rnd, k).start()

    def plane_copy(kx, ky):
        return pltpu.make_async_remote_copy(
            src_ref=p_send.at[kx * 4 + ky], dst_ref=p_recv.at[kx * 4 + ky],
            send_sem=p_sem.at[0], recv_sem=p_sem.at[1],
            device_id=device(zh, lax.rem(x + kx, 4), zl, lax.rem(y + ky, 4), c), device_id_type=MESH,
        )

    def plane(rnd):
        pair_copy(rnd).wait_recv()
        for kx in (2, 1, 3, 0):
            p_acc[kx] = both_cores(rnd, lax.rem(x + kx, 4))
            for ya in range(4):
                for za in range(4):
                    p_sum[kx, ya, pl.ds(za * LINE, LINE), :] = p_acc[kx, pl.ds(za * UNIT + ya * LINE, LINE), :]
                p_sum[kx, ya, pl.ds(UNIT, 8), :] = jnp.zeros((8, COL), F32)
            for ky in (2, 1, 3, 0):
                if kx or ky:
                    p_send[kx * 4 + ky] = p_sum[kx, lax.rem(y + ky, 4)].astype(BF16)
                    plane_copy(kx, ky).start()

    def plane_wait():
        return pltpu.make_async_remote_copy(
            src_ref=p_send.at[pl.ds(1, 15)], dst_ref=p_recv.at[pl.ds(1, 15)],
            send_sem=p_sem.at[0], recv_sem=p_sem.at[1], device_id=sibling, device_id_type=MESH,
        )

    def z_copy(rnd, kz, kc):
        za = lax.rem(zh + kz, 4)
        ca = lax.rem(c + kc, 2)
        return pltpu.make_async_remote_copy(
            src_ref=z_send.at[rnd, za * 2 + ca], dst_ref=z_recv.at[rnd, kz * 2 + off],
            send_sem=z_ssem.at[rnd], recv_sem=z_rsem.at[rnd],
            device_id=device(za, x, c, y, ca), device_id_type=MESH,
        )

    def along_z(rnd):
        if rnd == LAST:
            plane_wait().wait_recv()
            z_sum[rnd] = p_sum[0, y] + jnp.sum(p_recv[pl.ds(1, 15)].astype(F32), axis=0)
        else:
            for k in (1, 3, 2):
                y_copy(rnd, k).wait_recv()
            z_sum[rnd] = (
                y_sum[rnd, y] + y_recv[rnd, 0].astype(F32)
                + y_recv[rnd, 1].astype(F32) + y_recv[rnd, 2].astype(F32)
            )
        for b in range(8):
            z_send[rnd, b] = z_sum[rnd, pl.ds(OWN * b, 16), :].astype(BF16)
        for kz in (2, 1, 3, 0):
            for kc in (1, 0):
                if kz == 0 and kc == 0:
                    @pl.when(off == 0)
                    def _():
                        z_recv[rnd, 0] = z_send[rnd, zh * 2 + c]
                    @pl.when(off == 1)
                    def _():
                        z_copy(rnd, 0, 0).start()
                else:
                    z_copy(rnd, kz, kc).start()

    def z_wait(rnd, recv):
        def wait(first):
            copy = pltpu.make_async_remote_copy(
                src_ref=z_send.at[rnd, pl.ds(first, 8 - first)],
                dst_ref=z_recv.at[rnd, pl.ds(first, 8 - first)],
                send_sem=z_ssem.at[rnd], recv_sem=z_rsem.at[rnd],
                device_id=sibling, device_id_type=MESH,
            )
            if recv:
                copy.wait_recv()
            else:
                copy.wait_send()
        @pl.when(off == 0)
        def _():
            wait(1)
        @pl.when(off == 1)
        def _():
            wait(0)

    def finish(rnd):
        z_wait(rnd, True)
        result = jnp.sum(z_recv[rnd].astype(F32), axis=0)[:OWN] * factor
        if rnd == PROJ:
            proj_ref[...] = result
        else:
            conv_ref[pl.ds(rnd, OWN, stride=CHUNKS), :] = result

    def projection():
        grad = dot(mid[pl.ds(0, BINS), :], g_v[0], 0, 0)
        for w in range(1, WIN):
            grad = grad + dot(mid[pl.ds(w * BINS, BINS), :], g_v[w], 0, 0)
        for j in range(C // COL):
            total[PROJ, pl.ds(j, BN, stride=C // COL), :] = grad[:, j * COL:(j + 1) * COL]

    def block_output():
        for w in range(WIN):
            rows = pl.ds(w * BINS, BINS)
            out_v[w] = (x_v[w].astype(F32) + dot(mid[rows, :], p_v[...])).astype(BF16)

    def outer_taps(ch):
        first = WIN - 1
        for w in range(WIN):
            wait_halo(dup_recv, dup_sem, ch, w)
            wait_halo(dlo_recv, dlo_sem, ch, w)
            clear_if(s < 2, dlo_recv, ch, w)
            clear_if(s >= 62, dup_recv, ch, w)
            if w < first - 1:
                continue
            rows = pl.ds(0, first * BINS) if w == first - 1 else pl.ds(w * BINS, BINS)
            both = jnp.concatenate([dup_recv[ch, rows, :], dlo_recv[ch, rows, :]], axis=1)
            for m in range(WIN):
                term = dot(act_t[pl.ds(m * BINS, BINS), rows], both)
                low, high = pl.ds(m * BINS, BINS), pl.ds(2 * C + m * BINS, BINS)
                if w == first - 1:
                    total[ch, low, :] = term[:, :COL]
                    total[ch, high, :] = term[:, COL:]
                else:
                    total[ch, low, :] = total[ch, low, :] + term[:, :COL]
                    total[ch, high, :] = total[ch, high, :] + term[:, COL:]

    def input_side(ch):
        cols = pl.ds(ch * COL, COL)
        for w in range(WIN):
            rows = pl.ds(w * BINS, BINS)
            term = (
                dot(dup_recv[ch, rows, :], w_v[0, :, cols], 1, 1)
                + dot(d_send[ch, rows, :], w_v[1, :, cols], 1, 1)
                + dot(dlo_recv[ch, rows, :], w_v[2, :, cols], 1, 1)
            )
            if ch:
                term = term + dact[rows, :]
            if ch < CHUNKS - 1:
                dact[rows, :] = term
            else:
                dx_v[w] = (g_v[w].astype(F32) + term * slope_x[rows, :]).astype(BF16)

    middle(0)
    send_products(2)
    centre_tap(0)
    middle(1)
    centre_tap(1)
    outer_taps(0)
    stage_a(0)
    input_side(0)
    ring(0, 0)
    middle(2)
    centre_tap(2)
    ring(0, 1)
    projection()
    stage_a(PROJ)
    block_output()
    ring(PROJ, 0)
    ring(0, 2)
    outer_taps(1)
    stage_a(1)
    ring(PROJ, 1)
    input_side(1)
    straight(1)
    ring(PROJ, 2)
    outer_taps(2)
    stage_a(2)
    along_y(0)
    plane(2)
    along_y(PROJ)
    along_y(1)
    input_side(2)
    along_z(0)
    along_z(PROJ)
    along_z(1)
    along_z(2)
    finish(0)
    finish(PROJ)
    finish(1)

    for i, (ref, to) in enumerate(((u_send, upper), (v_send, lower), (d_send, upper), (d_send, lower))):
        pltpu.make_async_remote_copy(
            src_ref=ref, dst_ref=ref, send_sem=ph_send_sem.at[i], recv_sem=u_sem.at[0, 0],
            device_id=to, device_id_type=MESH,
        ).wait_send()
    for rnd in range(ROUNDS):
        pair_copy(rnd).wait_send()
        if rnd == LAST:
            plane_wait().wait_send()
        else:
            for k in (1, 2, 3):
                x_copy(rnd, k).wait_send()
                y_copy(rnd, k).wait_send()
        z_wait(rnd, False)
    finish(LAST)


def write_out(*refs):
    *refs, sem = refs
    copies = [pltpu.make_async_copy(refs[i], refs[4 + i], sem.at[i]) for i in range(4)]
    for copy in copies:
        copy.start()
    for copy in copies:
        copy.wait()


def local(inputs, dilated_tap_weight, proj_weight, cotangent):
    total_rows = inputs.shape[0] * lax.axis_size("dp") * inputs.shape[1] * lax.axis_size("seq")
    factor = 1.0 / math.sqrt(total_rows)
    vm = pltpu.VMEM
    dma = pltpu.SemaphoreType.DMA
    halo = (CHUNKS, ROWS, COL)
    hbm = pl.BlockSpec(memory_space=pl.ANY)
    vmem = pl.BlockSpec(memory_space=pltpu.VMEM)
    results = pl.pallas_call(
        functools.partial(kernel, factor),
        out_shape=(
            vm(inputs.shape, BF16), vm(inputs.shape, BF16), vm((CHUNKS * OWN, COL), F32), vm((OWN, COL), F32),
        ),
        in_specs=[hbm] * 4,
        out_specs=(vmem,) * 4,
        scratch_shapes=[
            vm((WIN, BINS, C), BF16), vm((3, C, BN), BF16), vm((BN, C), BF16), vm((WIN, BINS, C), BF16),
            vm((ROWS, C), BF16), vm((C, ROWS), BF16), vm((ROWS, C), F32),
            vm((ROWS, BN), F32), vm((ROWS, BN), F32), vm((ROWS, BN), BF16), vm((ROWS, C), F32),
            vm(halo, BF16), vm(halo, BF16), vm(halo, BF16), vm(halo, BF16),
            vm(halo, BF16), vm(halo, BF16), vm(halo, BF16),
            vm((ROUNDS, ALL, COL), F32),
            vm((ROUNDS, 4 * PART, COL), BF16), vm((ROUNDS, 4 * PART, COL), BF16),
            vm((ROUNDS, 3, PART, COL), BF16), vm((ROUNDS, 3, PART, COL), BF16),
            vm((ROUNDS, PART, COL), F32),
            vm((ROUNDS, 4, UNIT + 8, COL), F32),
            vm((ROUNDS, 3, UNIT + 8, COL), BF16), vm((ROUNDS, 3, UNIT + 8, COL), BF16),
            vm((ROUNDS, UNIT + 8, COL), F32),
            vm((ROUNDS, 8, 16, COL), BF16), vm((ROUNDS, 8, 16, COL), BF16),
            vm((4, PART, COL), F32), vm((4, 4, UNIT + 8, COL), F32),
            vm((16, UNIT + 8, COL), BF16), vm((16, UNIT + 8, COL), BF16),
            dma((8,)), dma((4,)),
            dma((CHUNKS, WIN)), dma((CHUNKS, WIN)), dma((CHUNKS, WIN)), dma((CHUNKS, WIN)),
            dma((ROUNDS,)), dma((ROUNDS,)), dma((ROUNDS, 3)), dma((ROUNDS, 3)),
            dma((ROUNDS, 3)), dma((ROUNDS, 3)),
            dma((ROUNDS,)), dma((ROUNDS,)), dma((2,)),
        ],
        compiler_params=pltpu.CompilerParams(
            collective_id=0, has_side_effects=True, vmem_limit_bytes=44 * 1024 * 1024
        ),
        name="block",
    )(*[pltpu.with_memory_space_constraint(a, pltpu.HBM)
        for a in (inputs, dilated_tap_weight, proj_weight, cotangent)])
    results = [pltpu.with_memory_space_constraint(r, pltpu.VMEM) for r in results]
    return pl.pallas_call(
        write_out,
        out_shape=tuple(jax.ShapeDtypeStruct(r.shape, r.dtype) for r in results),
        in_specs=[vmem] * 4,
        out_specs=(hbm,) * 4,
        scratch_shapes=[dma((4,))],
        name="write_out",
    )(*results)


def solution(mesh):
    return jax.shard_map(
        local,
        mesh=mesh,
        in_specs=(P("dp", "seq", None), P(), P(), P("dp", "seq", None)),
        out_specs=(
            P("dp", "seq", None),
            P("dp", "seq", None),
            P(("dp", "seq"), None),
            P(("dp", "seq"), None),
        ),
        check_vma=False,
    )
```

```python
import functools
import math

import jax
import jax.numpy as jnp
from jax import lax
from jax.experimental import pallas as pl
from jax.experimental.pallas import tpu as pltpu
from jax.sharding import PartitionSpec as P

MESH = pl.DeviceIdType.MESH
F32 = jnp.float32
BF16 = jnp.bfloat16
SLOPE = math.sqrt(2.0 / math.pi)
CUBIC = 0.044715

WIN = 3
BINS = 256
ROWS = WIN * BINS
C = 768
BN = 384
COL = 128
CHUNKS = BN // COL
PROJ = CHUNKS
ROUNDS = CHUNKS + 1
LAST = CHUNKS - 1
STRAIGHT = (LAST - 1, PROJ)
ALL = 2304
UNIT = 72
PART = 4 * UNIT
LINE = 18
OWN = 9


def gelu_parts(v):
    sq = v * v
    t = jnp.tanh(SLOPE * v * (1.0 + CUBIC * sq))
    half = 0.5 * (1.0 + t)
    value = v * half
    slope = half + (0.5 * SLOPE) * v * (1.0 - t * t) * (1.0 + (3.0 * CUBIC) * sq)
    return value, slope


def dot(a, b, ca=1, cb=0):
    return lax.dot_general(a, b, (((ca,), (cb,)), ((), ())), preferred_element_type=F32)


def kernel(
    factor,
    x_hbm, w_hbm, p_hbm, g_hbm,
    out_v, dx_v, conv_ref, proj_ref,
    x_v, w_v, p_v, g_v, act, act_t, slope_x, cpre, dmid, mid, dact,
    u_send, v_send, u_recv, v_recv, d_send, dup_recv, dlo_recv,
    total, pair_send, pair_recv, x_send, x_recv, acc,
    y_sum, y_send, y_recv, z_sum, z_send, z_recv,
    p_acc, p_sum, p_send, p_recv,
    in_sem, ph_send_sem, u_sem, v_sem, dup_sem, dlo_sem,
    pair_ssem, pair_rsem, x_ssem, x_rsem, y_ssem, y_rsem, z_ssem, z_rsem, p_sem,
):
    zh = lax.axis_index("dp")
    s = lax.axis_index("seq")
    x = s // 16
    zl = lax.rem(s // 8, 2)
    y = lax.rem(s // 2, 4)
    c = lax.rem(s, 2)
    off = lax.rem(zl + c, 2)

    def device(zh_, x_, zl_, y_, c_):
        return (zh_, ((x_ * 2 + zl_) * 4 + y_) * 2 + c_)

    upper = (zh, lax.rem(s + 2, 64))
    lower = (zh, lax.rem(s + 62, 64))
    sibling = device(zh, x, zl, y, 1 - c)

    loads = {}
    def load(name, src, dst, i):
        loads[name] = pltpu.make_async_copy(src, dst, in_sem.at[i])
        loads[name].start()
    load("x0", x_hbm.at[0], x_v.at[0], 0)
    load("w0", w_hbm.at[0], w_v.at[0], 3)
    load("w2", w_hbm.at[2], w_v.at[2], 5)
    load("x1", x_hbm.at[1], x_v.at[1], 1)
    load("x2", x_hbm.at[2], x_v.at[2], 2)
    load("w1", w_hbm.at[1], w_v.at[1], 4)
    load("p", p_hbm, p_v, 6)
    load("g", g_hbm, g_v, 7)

    barrier = pltpu.get_barrier_semaphore()
    def greet(peer):
        pl.semaphore_signal(barrier, inc=1, device_id=peer, device_id_type=MESH)
    greet(upper)
    greet(lower)
    greet(sibling)
    for k in (1, 2, 3):
        greet(device(zh, lax.rem(x + k, 4), zl, y, c))
        greet(device(zh, x, zl, lax.rem(y + k, 4), c))
        for j in (1, 2, 3):
            greet(device(zh, lax.rem(x + k, 4), zl, lax.rem(y + j, 4), c))
    for kz in range(4):
        for kl in range(2):
            peer = device(lax.rem(zh + kz, 4), x, lax.rem(zl + c + kl, 2), y, zl)
            if kz == 0:
                is_self = jnp.logical_and(lax.rem(c + kl, 2) == 0, c == zl)
                @pl.when(jnp.logical_not(is_self))
                def _(peer=peer):
                    greet(peer)
            else:
                greet(peer)

    def send_halo(src, dst, sem, ssem, ch, w, to):
        pltpu.make_async_remote_copy(
            src_ref=src.at[ch, pl.ds(w * BINS, BINS)],
            dst_ref=dst.at[ch, pl.ds(w * BINS, BINS)],
            send_sem=ph_send_sem.at[ssem],
            recv_sem=sem.at[ch, w],
            device_id=to,
            device_id_type=MESH,
        ).start()

    def wait_halo(dst, sem, ch, w):
        ref = dst.at[ch, pl.ds(w * BINS, BINS)]
        pltpu.make_async_remote_copy(
            src_ref=ref, dst_ref=ref, send_sem=ph_send_sem.at[0], recv_sem=sem.at[ch, w],
            device_id=upper, device_id_type=MESH,
        ).wait_recv()

    SLAB = 16
    for w in range(WIN):
        loads["x%d" % w].wait()
        def activate(i, carry, w=w):
            r = pl.multiple_of(i * SLAB, SLAB)
            v = x_v[w, pl.ds(r, SLAB), :].astype(F32)
            value, slope = gelu_parts(v)
            act[pl.ds(w * BINS + r, SLAB), :] = value.astype(BF16)
            slope_x[pl.ds(w * BINS + r, SLAB), :] = slope
            return carry
        lax.fori_loop(0, BINS // SLAB, activate, 0)
        a_w = act[pl.ds(w * BINS, BINS), :]
        if w == 0:
            loads["w0"].wait()
        u = dot(a_w, w_v[0]).astype(BF16)
        for ch in range(CHUNKS):
            u_send[ch, pl.ds(w * BINS, BINS), :] = u[:, ch * COL:(ch + 1) * COL]
        if w == 0:
            pl.semaphore_wait(barrier, 2 + 1 + 15 + 7 + off)
        send_halo(u_send, u_recv, u_sem, 0, 0, w, upper)
        if w == 0:
            loads["w2"].wait()
        v = dot(a_w, w_v[2]).astype(BF16)
        for ch in range(CHUNKS):
            v_send[ch, pl.ds(w * BINS, BINS), :] = v[:, ch * COL:(ch + 1) * COL]
        send_halo(v_send, v_recv, v_sem, 1, 0, w, lower)

    def send_products(ch):
        for w in range(WIN):
            send_halo(u_send, u_recv, u_sem, 0, ch, w, upper)
            send_halo(v_send, v_recv, v_sem, 1, ch, w, lower)

    send_products(1)

    loads["w1"].wait()
    loads["p"].wait()
    loads["g"].wait()
    for w in range(WIN):
        rows = pl.ds(w * BINS, BINS)
        cpre[rows, :] = dot(act[rows, :], w_v[1])
        dmid[rows, :] = dot(g_v[w], p_v[...], 1, 1)
        act_t[:, rows] = act[rows, :].T

    def clear_if(cond, ref, ch, w):
        @pl.when(cond)
        def _():
            ref[ch, pl.ds(w * BINS, BINS), :] = jnp.zeros((BINS, COL), BF16)

    MIDSLAB = 64
    def middle(ch):
        for w in range(WIN):
            wait_halo(u_recv, u_sem, ch, w)
            wait_halo(v_recv, v_sem, ch, w)
            clear_if(s < 2, u_recv, ch, w)
            clear_if(s >= 62, v_recv, ch, w)
            def bottleneck(i, carry, w=w):
                r = pl.multiple_of(w * BINS + i * MIDSLAB, MIDSLAB)
                rows = pl.ds(r, MIDSLAB)
                cols = pl.ds(ch * COL, COL)
                pre = cpre[rows, cols] + u_recv[ch, rows, :].astype(F32) + v_recv[ch, rows, :].astype(F32)
                value, slope = gelu_parts(pre)
                mid[rows, cols] = value.astype(BF16)
                d_send[ch, rows, :] = (dmid[rows, cols] * slope).astype(BF16)
                return carry
            lax.fori_loop(0, BINS // MIDSLAB, bottleneck, 0)
            send_halo(d_send, dlo_recv, dlo_sem, 2, ch, w, upper)
            send_halo(d_send, dup_recv, dup_sem, 3, ch, w, lower)

    def centre_tap(ch):
        total[ch, pl.ds(C, C), :] = dot(act_t[...], d_send[ch])

    def unit(rnd, zh_, x_, zl_):
        start = pl.multiple_of((zh_ * 8 + x_ * 2 + zl_) * UNIT, 8)
        return total[rnd, pl.ds(start, UNIT), :]

    def part(rnd, x_, zl_):
        return jnp.concatenate([unit(rnd, k, x_, zl_) for k in range(4)], axis=0)

    def part_rows(k):
        return pl.ds(pl.multiple_of(lax.rem(x + k, 4) * PART, 16), PART)

    def pair_copy(rnd, k):
        return pltpu.make_async_remote_copy(
            src_ref=pair_send.at[rnd, part_rows(k)], dst_ref=pair_recv.at[rnd, part_rows(k)],
            send_sem=pair_ssem.at[rnd, k], recv_sem=pair_rsem.at[rnd, k],
            device_id=sibling, device_id_type=MESH,
        )

    def stage_a(rnd):
        for k in (2, 1, 3, 0):
            pair_send[rnd, part_rows(k), :] = part(rnd, lax.rem(x + k, 4), 1 - c).astype(BF16)
            pair_copy(rnd, k).start()

    def pair_wait(rnd):
        for k in range(4):
            pair_copy(rnd, k).wait_recv()

    def x_copy(rnd, k):
        return pltpu.make_async_remote_copy(
            src_ref=x_send.at[rnd, k - 1], dst_ref=x_recv.at[rnd, k - 1],
            send_sem=x_ssem.at[rnd, k - 1], recv_sem=x_rsem.at[rnd, k - 1],
            device_id=device(zh, lax.rem(x + k, 4), zl, y, c), device_id_type=MESH,
        )

    def both_cores(rnd, xa):
        other = pair_recv[rnd, pl.ds(pl.multiple_of(xa * PART, 16), PART), :]
        return part(rnd, xa, c) + other.astype(F32)

    step = jnp.where(zl == 1, 1, 3)

    def ring_copy(rnd, t):
        return pltpu.make_async_remote_copy(
            src_ref=x_send.at[rnd, t], dst_ref=x_recv.at[rnd, t],
            send_sem=x_ssem.at[rnd, t], recv_sem=x_rsem.at[rnd, t],
            device_id=device(zh, lax.rem(x + step, 4), zl, y, c), device_id_type=MESH,
        )

    def ring(rnd, t):
        if t == 0:
            pair_wait(rnd)
            part_sum = both_cores(rnd, lax.rem(x + 4 - step, 4))
        else:
            ring_copy(rnd, t - 1).wait_recv()
            xa = lax.rem(x + 2, 4) if t == 1 else lax.rem(x + step, 4)
            part_sum = both_cores(rnd, xa) + x_recv[rnd, t - 1].astype(F32)
        x_send[rnd, t] = part_sum.astype(BF16)
        ring_copy(rnd, t).start()

    def straight(rnd):
        pair_wait(rnd)
        for k in (2, 1, 3):
            x_send[rnd, k - 1] = both_cores(rnd, lax.rem(x + k, 4)).astype(BF16)
            x_copy(rnd, k).start()

    def y_copy(rnd, k):
        return pltpu.make_async_remote_copy(
            src_ref=y_send.at[rnd, k - 1], dst_ref=y_recv.at[rnd, k - 1],
            send_sem=y_ssem.at[rnd, k - 1], recv_sem=y_rsem.at[rnd, k - 1],
            device_id=device(zh, x, zl, lax.rem(y + k, 4), c), device_id_type=MESH,
        )

    def along_y(rnd):
        mine = both_cores(rnd, x)
        if rnd in STRAIGHT:
            for k in (1, 3, 2):
                x_copy(rnd, k).wait_recv()
            mine = mine + x_recv[rnd, 0].astype(F32) + x_recv[rnd, 1].astype(F32)
        else:
            ring_copy(rnd, 2).wait_recv()
        acc[rnd] = mine + x_recv[rnd, 2].astype(F32)
        for ya in range(4):
            for za in range(4):
                y_sum[rnd, ya, pl.ds(za * LINE, LINE), :] = acc[rnd, pl.ds(za * UNIT + ya * LINE, LINE), :]
            y_sum[rnd, ya, pl.ds(UNIT, 8), :] = jnp.zeros((8, COL), F32)
        for k in (2, 1, 3):
            y_send[rnd, k - 1] = y_sum[rnd, lax.rem(y + k, 4)].astype(BF16)
            y_copy(rnd, k).start()

    def plane_copy(kx, ky):
        return pltpu.make_async_remote_copy(
            src_ref=p_send.at[kx * 4 + ky], dst_ref=p_recv.at[kx * 4 + ky],
            send_sem=p_sem.at[0], recv_sem=p_sem.at[1],
            device_id=device(zh, lax.rem(x + kx, 4), zl, lax.rem(y + ky, 4), c), device_id_type=MESH,
        )

    def plane(rnd):
        for kx in (2, 1, 3, 0):
            pair_copy(rnd, kx).wait_recv()
            p_acc[kx] = both_cores(rnd, lax.rem(x + kx, 4))
            for ya in range(4):
                for za in range(4):
                    p_sum[kx, ya, pl.ds(za * LINE, LINE), :] = p_acc[kx, pl.ds(za * UNIT + ya * LINE, LINE), :]
                p_sum[kx, ya, pl.ds(UNIT, 8), :] = jnp.zeros((8, COL), F32)
            for ky in (2, 1, 3, 0):
                if kx or ky:
                    p_send[kx * 4 + ky] = p_sum[kx, lax.rem(y + ky, 4)].astype(BF16)
                    plane_copy(kx, ky).start()

    def plane_wait():
        return pltpu.make_async_remote_copy(
            src_ref=p_send.at[pl.ds(1, 15)], dst_ref=p_recv.at[pl.ds(1, 15)],
            send_sem=p_sem.at[0], recv_sem=p_sem.at[1], device_id=sibling, device_id_type=MESH,
        )

    def z_copy(rnd, kz, kc):
        za = lax.rem(zh + kz, 4)
        ca = lax.rem(c + kc, 2)
        return pltpu.make_async_remote_copy(
            src_ref=z_send.at[rnd, za * 2 + ca], dst_ref=z_recv.at[rnd, kz * 2 + off],
            send_sem=z_ssem.at[rnd], recv_sem=z_rsem.at[rnd],
            device_id=device(za, x, c, y, ca), device_id_type=MESH,
        )

    def along_z(rnd):
        if rnd == LAST:
            plane_wait().wait_recv()
            z_sum[rnd] = p_sum[0, y] + jnp.sum(p_recv[pl.ds(1, 15)].astype(F32), axis=0)
        else:
            for k in (1, 3, 2):
                y_copy(rnd, k).wait_recv()
            z_sum[rnd] = (
                y_sum[rnd, y] + y_recv[rnd, 0].astype(F32)
                + y_recv[rnd, 1].astype(F32) + y_recv[rnd, 2].astype(F32)
            )
        for b in range(8):
            z_send[rnd, b] = z_sum[rnd, pl.ds(OWN * b, 16), :].astype(BF16)
        for kz in (2, 1, 3, 0):
            for kc in (1, 0):
                if kz == 0 and kc == 0:
                    @pl.when(off == 0)
                    def _():
                        z_recv[rnd, 0] = z_send[rnd, zh * 2 + c]
                    @pl.when(off == 1)
                    def _():
                        z_copy(rnd, 0, 0).start()
                else:
                    z_copy(rnd, kz, kc).start()

    def z_wait(rnd, recv):
        def wait(first):
            copy = pltpu.make_async_remote_copy(
                src_ref=z_send.at[rnd, pl.ds(first, 8 - first)],
                dst_ref=z_recv.at[rnd, pl.ds(first, 8 - first)],
                send_sem=z_ssem.at[rnd], recv_sem=z_rsem.at[rnd],
                device_id=sibling, device_id_type=MESH,
            )
            if recv:
                copy.wait_recv()
            else:
                copy.wait_send()
        @pl.when(off == 0)
        def _():
            wait(1)
        @pl.when(off == 1)
        def _():
            wait(0)

    def finish(rnd):
        z_wait(rnd, True)
        result = jnp.sum(z_recv[rnd].astype(F32), axis=0)[:OWN] * factor
        if rnd == PROJ:
            proj_ref[...] = result
        else:
            conv_ref[pl.ds(rnd, OWN, stride=CHUNKS), :] = result

    def projection():
        grad = dot(mid[pl.ds(0, BINS), :], g_v[0], 0, 0)
        for w in range(1, WIN):
            grad = grad + dot(mid[pl.ds(w * BINS, BINS), :], g_v[w], 0, 0)
        for j in range(C // COL):
            total[PROJ, pl.ds(j, BN, stride=C // COL), :] = grad[:, j * COL:(j + 1) * COL]

    def block_output():
        for w in range(WIN):
            rows = pl.ds(w * BINS, BINS)
            out_v[w] = (x_v[w].astype(F32) + dot(mid[rows, :], p_v[...])).astype(BF16)

    def outer_taps(ch):
        first = WIN - 1
        for w in range(WIN):
            wait_halo(dup_recv, dup_sem, ch, w)
            wait_halo(dlo_recv, dlo_sem, ch, w)
            clear_if(s < 2, dlo_recv, ch, w)
            clear_if(s >= 62, dup_recv, ch, w)
            if w < first - 1:
                continue
            rows = pl.ds(0, first * BINS) if w == first - 1 else pl.ds(w * BINS, BINS)
            both = jnp.concatenate([dup_recv[ch, rows, :], dlo_recv[ch, rows, :]], axis=1)
            for m in range(WIN):
                term = dot(act_t[pl.ds(m * BINS, BINS), rows], both)
                low, high = pl.ds(m * BINS, BINS), pl.ds(2 * C + m * BINS, BINS)
                if w == first - 1:
                    total[ch, low, :] = term[:, :COL]
                    total[ch, high, :] = term[:, COL:]
                else:
                    total[ch, low, :] = total[ch, low, :] + term[:, :COL]
                    total[ch, high, :] = total[ch, high, :] + term[:, COL:]

    def input_side(ch):
        cols = pl.ds(ch * COL, COL)
        for w in range(WIN):
            rows = pl.ds(w * BINS, BINS)
            term = (
                dot(dup_recv[ch, rows, :], w_v[0, :, cols], 1, 1)
                + dot(d_send[ch, rows, :], w_v[1, :, cols], 1, 1)
                + dot(dlo_recv[ch, rows, :], w_v[2, :, cols], 1, 1)
            )
            if ch:
                term = term + dact[rows, :]
            if ch < CHUNKS - 1:
                dact[rows, :] = term
            else:
                dx_v[w] = (g_v[w].astype(F32) + term * slope_x[rows, :]).astype(BF16)

    middle(0)
    send_products(2)
    centre_tap(0)
    middle(1)
    centre_tap(1)
    outer_taps(0)
    stage_a(0)
    input_side(0)
    ring(0, 0)
    middle(2)
    centre_tap(2)
    ring(0, 1)
    projection()
    stage_a(PROJ)
    block_output()
    straight(PROJ)
    ring(0, 2)
    outer_taps(1)
    stage_a(1)
    input_side(1)
    straight(1)
    outer_taps(2)
    stage_a(2)
    along_y(0)
    plane(2)
    along_y(PROJ)
    along_y(1)
    input_side(2)
    along_z(0)
    along_z(PROJ)
    along_z(1)
    along_z(2)
    finish(0)
    finish(PROJ)
    finish(1)

    for i, (ref, to) in enumerate(((u_send, upper), (v_send, lower), (d_send, upper), (d_send, lower))):
        pltpu.make_async_remote_copy(
            src_ref=ref, dst_ref=ref, send_sem=ph_send_sem.at[i], recv_sem=u_sem.at[0, 0],
            device_id=to, device_id_type=MESH,
        ).wait_send()
    for rnd in range(ROUNDS):
        for k in range(4):
            pair_copy(rnd, k).wait_send()
        if rnd == LAST:
            plane_wait().wait_send()
        else:
            for k in (1, 2, 3):
                x_copy(rnd, k).wait_send()
                y_copy(rnd, k).wait_send()
        z_wait(rnd, False)
    finish(LAST)


def write_out(*refs):
    *refs, sem = refs
    copies = [pltpu.make_async_copy(refs[i], refs[4 + i], sem.at[i]) for i in range(4)]
    for copy in copies:
        copy.start()
    for copy in copies:
        copy.wait()


def local(inputs, dilated_tap_weight, proj_weight, cotangent):
    total_rows = inputs.shape[0] * lax.axis_size("dp") * inputs.shape[1] * lax.axis_size("seq")
    factor = 1.0 / math.sqrt(total_rows)
    vm = pltpu.VMEM
    dma = pltpu.SemaphoreType.DMA
    halo = (CHUNKS, ROWS, COL)
    hbm = pl.BlockSpec(memory_space=pl.ANY)
    vmem = pl.BlockSpec(memory_space=pltpu.VMEM)
    results = pl.pallas_call(
        functools.partial(kernel, factor),
        out_shape=(
            vm(inputs.shape, BF16), vm(inputs.shape, BF16), vm((CHUNKS * OWN, COL), F32), vm((OWN, COL), F32),
        ),
        in_specs=[hbm] * 4,
        out_specs=(vmem,) * 4,
        scratch_shapes=[
            vm((WIN, BINS, C), BF16), vm((3, C, BN), BF16), vm((BN, C), BF16), vm((WIN, BINS, C), BF16),
            vm((ROWS, C), BF16), vm((C, ROWS), BF16), vm((ROWS, C), F32),
            vm((ROWS, BN), F32), vm((ROWS, BN), F32), vm((ROWS, BN), BF16), vm((ROWS, C), F32),
            vm(halo, BF16), vm(halo, BF16), vm(halo, BF16), vm(halo, BF16),
            vm(halo, BF16), vm(halo, BF16), vm(halo, BF16),
            vm((ROUNDS, ALL, COL), F32),
            vm((ROUNDS, 4 * PART, COL), BF16), vm((ROUNDS, 4 * PART, COL), BF16),
            vm((ROUNDS, 3, PART, COL), BF16), vm((ROUNDS, 3, PART, COL), BF16),
            vm((ROUNDS, PART, COL), F32),
            vm((ROUNDS, 4, UNIT + 8, COL), F32),
            vm((ROUNDS, 3, UNIT + 8, COL), BF16), vm((ROUNDS, 3, UNIT + 8, COL), BF16),
            vm((ROUNDS, UNIT + 8, COL), F32),
            vm((ROUNDS, 8, 16, COL), BF16), vm((ROUNDS, 8, 16, COL), BF16),
            vm((4, PART, COL), F32), vm((4, 4, UNIT + 8, COL), F32),
            vm((16, UNIT + 8, COL), BF16), vm((16, UNIT + 8, COL), BF16),
            dma((8,)), dma((4,)),
            dma((CHUNKS, WIN)), dma((CHUNKS, WIN)), dma((CHUNKS, WIN)), dma((CHUNKS, WIN)),
            dma((ROUNDS, 4)), dma((ROUNDS, 4)), dma((ROUNDS, 3)), dma((ROUNDS, 3)),
            dma((ROUNDS, 3)), dma((ROUNDS, 3)),
            dma((ROUNDS,)), dma((ROUNDS,)), dma((2,)),
        ],
        compiler_params=pltpu.CompilerParams(
            collective_id=0, has_side_effects=True, vmem_limit_bytes=44 * 1024 * 1024
        ),
        name="block",
    )(*[pltpu.with_memory_space_constraint(a, pltpu.HBM)
        for a in (inputs, dilated_tap_weight, proj_weight, cotangent)])
    results = [pltpu.with_memory_space_constraint(r, pltpu.VMEM) for r in results]
    return pl.pallas_call(
        write_out,
        out_shape=tuple(jax.ShapeDtypeStruct(r.shape, r.dtype) for r in results),
        in_specs=[vmem] * 4,
        out_specs=(hbm,) * 4,
        scratch_shapes=[dma((4,))],
        name="write_out",
    )(*results)


def solution(mesh):
    return jax.shard_map(
        local,
        mesh=mesh,
        in_specs=(P("dp", "seq", None), P(), P(), P("dp", "seq", None)),
        out_specs=(
            P("dp", "seq", None),
            P("dp", "seq", None),
            P(("dp", "seq"), None),
            P(("dp", "seq"), None),
        ),
        check_vma=False,
    )
```

```python
import functools
import math

import jax
import jax.numpy as jnp
from jax import lax
from jax.experimental import pallas as pl
from jax.experimental.pallas import tpu as pltpu
from jax.sharding import PartitionSpec as P

MESH = pl.DeviceIdType.MESH
F32 = jnp.float32
BF16 = jnp.bfloat16
SLOPE = math.sqrt(2.0 / math.pi)
CUBIC = 0.044715

WIN = 3
BINS = 256
ROWS = WIN * BINS
C = 768
BN = 384
COL = 128
CHUNKS = BN // COL
PROJ = CHUNKS
ROUNDS = CHUNKS + 1
LAST = CHUNKS - 1
STRAIGHT = (LAST - 1, PROJ)
ALL = 2304
UNIT = 72
PART = 4 * UNIT
LINE = 18
OWN = 9


def gelu_parts(v):
    sq = v * v
    t = jnp.tanh(SLOPE * v * (1.0 + CUBIC * sq))
    half = 0.5 * (1.0 + t)
    value = v * half
    slope = half + (0.5 * SLOPE) * v * (1.0 - t * t) * (1.0 + (3.0 * CUBIC) * sq)
    return value, slope


def dot(a, b, ca=1, cb=0):
    return lax.dot_general(a, b, (((ca,), (cb,)), ((), ())), preferred_element_type=F32)


def kernel(
    factor,
    x_hbm, w_hbm, p_hbm, g_hbm,
    out_v, dx_v, conv_ref, proj_ref,
    x_v, w_v, p_v, g_v, act, act_t, slope_x, cpre, dmid, mid, dact,
    u_send, v_send, u_recv, v_recv, d_send, dup_recv, dlo_recv,
    total, pair_send, pair_recv, x_send, x_recv, acc,
    y_sum, y_send, y_recv, z_sum, z_send, z_recv,
    p_acc, p_sum, p_send, p_recv,
    in_sem, ph_send_sem, u_sem, v_sem, dup_sem, dlo_sem,
    pair_ssem, pair_rsem, x_ssem, x_rsem, y_ssem, y_rsem, z_ssem, z_rsem, p_sem,
):
    zh = lax.axis_index("dp")
    s = lax.axis_index("seq")
    x = s // 16
    zl = lax.rem(s // 8, 2)
    y = lax.rem(s // 2, 4)
    c = lax.rem(s, 2)
    off = lax.rem(zl + c, 2)

    def device(zh_, x_, zl_, y_, c_):
        return (zh_, ((x_ * 2 + zl_) * 4 + y_) * 2 + c_)

    upper = (zh, lax.rem(s + 2, 64))
    lower = (zh, lax.rem(s + 62, 64))
    sibling = device(zh, x, zl, y, 1 - c)

    loads = {}
    def load(name, src, dst, i):
        loads[name] = pltpu.make_async_copy(src, dst, in_sem.at[i])
        loads[name].start()
    load("x0", x_hbm.at[0], x_v.at[0], 0)
    load("w0", w_hbm.at[0], w_v.at[0], 3)
    load("w2", w_hbm.at[2], w_v.at[2], 5)
    load("x1", x_hbm.at[1], x_v.at[1], 1)
    load("x2", x_hbm.at[2], x_v.at[2], 2)
    load("w1", w_hbm.at[1], w_v.at[1], 4)
    load("p", p_hbm, p_v, 6)
    load("g", g_hbm, g_v, 7)

    barrier = pltpu.get_barrier_semaphore()
    def greet(peer):
        pl.semaphore_signal(barrier, inc=1, device_id=peer, device_id_type=MESH)
    greet(upper)
    greet(lower)
    greet(sibling)
    for k in (1, 2, 3):
        greet(device(zh, lax.rem(x + k, 4), zl, y, c))
        greet(device(zh, x, zl, lax.rem(y + k, 4), c))
        for j in (1, 2, 3):
            greet(device(zh, lax.rem(x + k, 4), zl, lax.rem(y + j, 4), c))
    for kz in range(4):
        for kl in range(2):
            peer = device(lax.rem(zh + kz, 4), x, lax.rem(zl + c + kl, 2), y, zl)
            if kz == 0:
                is_self = jnp.logical_and(lax.rem(c + kl, 2) == 0, c == zl)
                @pl.when(jnp.logical_not(is_self))
                def _(peer=peer):
                    greet(peer)
            else:
                greet(peer)

    def send_halo(src, dst, sem, ssem, ch, w, to):
        pltpu.make_async_remote_copy(
            src_ref=src.at[ch, pl.ds(w * BINS, BINS)],
            dst_ref=dst.at[ch, pl.ds(w * BINS, BINS)],
            send_sem=ph_send_sem.at[ssem],
            recv_sem=sem.at[ch, w],
            device_id=to,
            device_id_type=MESH,
        ).start()

    def wait_halo(dst, sem, ch, w):
        ref = dst.at[ch, pl.ds(w * BINS, BINS)]
        pltpu.make_async_remote_copy(
            src_ref=ref, dst_ref=ref, send_sem=ph_send_sem.at[0], recv_sem=sem.at[ch, w],
            device_id=upper, device_id_type=MESH,
        ).wait_recv()

    SLAB = 16
    for w in range(WIN):
        loads["x%d" % w].wait()
        def activate(i, carry, w=w):
            r = pl.multiple_of(i * SLAB, SLAB)
            v = x_v[w, pl.ds(r, SLAB), :].astype(F32)
            value, slope = gelu_parts(v)
            act[pl.ds(w * BINS + r, SLAB), :] = value.astype(BF16)
            slope_x[pl.ds(w * BINS + r, SLAB), :] = slope
            return carry
        lax.fori_loop(0, BINS // SLAB, activate, 0)
        a_w = act[pl.ds(w * BINS, BINS), :]
        if w == 0:
            loads["w0"].wait()
        u = dot(a_w, w_v[0]).astype(BF16)
        for ch in range(CHUNKS):
            u_send[ch, pl.ds(w * BINS, BINS), :] = u[:, ch * COL:(ch + 1) * COL]
        if w == 0:
            pl.semaphore_wait(barrier, 2 + 1 + 15 + 7 + off)
        send_halo(u_send, u_recv, u_sem, 0, 0, w, upper)
        if w == 0:
            loads["w2"].wait()
        v = dot(a_w, w_v[2]).astype(BF16)
        for ch in range(CHUNKS):
            v_send[ch, pl.ds(w * BINS, BINS), :] = v[:, ch * COL:(ch + 1) * COL]
        send_halo(v_send, v_recv, v_sem, 1, 0, w, lower)

    def send_products(ch):
        for w in range(WIN):
            send_halo(u_send, u_recv, u_sem, 0, ch, w, upper)
            send_halo(v_send, v_recv, v_sem, 1, ch, w, lower)

    send_products(1)

    loads["w1"].wait()
    loads["p"].wait()
    loads["g"].wait()
    for w in range(WIN):
        rows = pl.ds(w * BINS, BINS)
        cpre[rows, :] = dot(act[rows, :], w_v[1])
        dmid[rows, :] = dot(g_v[w], p_v[...], 1, 1)
        act_t[:, rows] = act[rows, :].T

    def clear_if(cond, ref, ch, w):
        @pl.when(cond)
        def _():
            ref[ch, pl.ds(w * BINS, BINS), :] = jnp.zeros((BINS, COL), BF16)

    MIDSLAB = 64
    def middle(ch):
        for w in range(WIN):
            wait_halo(u_recv, u_sem, ch, w)
            wait_halo(v_recv, v_sem, ch, w)
            clear_if(s < 2, u_recv, ch, w)
            clear_if(s >= 62, v_recv, ch, w)
            def bottleneck(i, carry, w=w):
                r = pl.multiple_of(w * BINS + i * MIDSLAB, MIDSLAB)
                rows = pl.ds(r, MIDSLAB)
                cols = pl.ds(ch * COL, COL)
                pre = cpre[rows, cols] + u_recv[ch, rows, :].astype(F32) + v_recv[ch, rows, :].astype(F32)
                value, slope = gelu_parts(pre)
                mid[rows, cols] = value.astype(BF16)
                d_send[ch, rows, :] = (dmid[rows, cols] * slope).astype(BF16)
                return carry
            lax.fori_loop(0, BINS // MIDSLAB, bottleneck, 0)
            send_halo(d_send, dlo_recv, dlo_sem, 2, ch, w, upper)
            send_halo(d_send, dup_recv, dup_sem, 3, ch, w, lower)

    def centre_tap(ch):
        total[ch, pl.ds(C, C), :] = dot(act_t[...], d_send[ch])

    def unit(rnd, zh_, x_, zl_):
        start = pl.multiple_of((zh_ * 8 + x_ * 2 + zl_) * UNIT, 8)
        return total[rnd, pl.ds(start, UNIT), :]

    def part(rnd, x_, zl_):
        return jnp.concatenate([unit(rnd, k, x_, zl_) for k in range(4)], axis=0)

    def part_rows(k):
        return pl.ds(pl.multiple_of(lax.rem(x + k, 4) * PART, 16), PART)

    def pair_copy(rnd, k):
        return pltpu.make_async_remote_copy(
            src_ref=pair_send.at[rnd, part_rows(k)], dst_ref=pair_recv.at[rnd, part_rows(k)],
            send_sem=pair_ssem.at[rnd, k], recv_sem=pair_rsem.at[rnd, k],
            device_id=sibling, device_id_type=MESH,
        )

    def stage_a(rnd):
        for k in (2, 1, 3, 0):
            pair_send[rnd, part_rows(k), :] = part(rnd, lax.rem(x + k, 4), 1 - c).astype(BF16)
            pair_copy(rnd, k).start()

    def pair_wait(rnd):
        for k in range(4):
            pair_copy(rnd, k).wait_recv()

    def x_copy(rnd, k):
        return pltpu.make_async_remote_copy(
            src_ref=x_send.at[rnd, k - 1], dst_ref=x_recv.at[rnd, k - 1],
            send_sem=x_ssem.at[rnd, k - 1], recv_sem=x_rsem.at[rnd, k - 1],
            device_id=device(zh, lax.rem(x + k, 4), zl, y, c), device_id_type=MESH,
        )

    def both_cores(rnd, xa):
        other = pair_recv[rnd, pl.ds(pl.multiple_of(xa * PART, 16), PART), :]
        return part(rnd, xa, c) + other.astype(F32)

    step = jnp.where(zl == 1, 1, 3)

    def ring_copy(rnd, t):
        return pltpu.make_async_remote_copy(
            src_ref=x_send.at[rnd, t], dst_ref=x_recv.at[rnd, t],
            send_sem=x_ssem.at[rnd, t], recv_sem=x_rsem.at[rnd, t],
            device_id=device(zh, lax.rem(x + step, 4), zl, y, c), device_id_type=MESH,
        )

    def ring(rnd, t):
        if t == 0:
            pair_wait(rnd)
            part_sum = both_cores(rnd, lax.rem(x + 4 - step, 4))
        else:
            ring_copy(rnd, t - 1).wait_recv()
            xa = lax.rem(x + 2, 4) if t == 1 else lax.rem(x + step, 4)
            part_sum = both_cores(rnd, xa) + x_recv[rnd, t - 1].astype(F32)
        x_send[rnd, t] = part_sum.astype(BF16)
        ring_copy(rnd, t).start()

    def straight(rnd):
        pair_wait(rnd)
        for k in (2, 1, 3):
            x_send[rnd, k - 1] = both_cores(rnd, lax.rem(x + k, 4)).astype(BF16)
            x_copy(rnd, k).start()

    def y_copy(rnd, k):
        return pltpu.make_async_remote_copy(
            src_ref=y_send.at[rnd, k - 1], dst_ref=y_recv.at[rnd, k - 1],
            send_sem=y_ssem.at[rnd, k - 1], recv_sem=y_rsem.at[rnd, k - 1],
            device_id=device(zh, x, zl, lax.rem(y + k, 4), c), device_id_type=MESH,
        )

    def along_y(rnd):
        mine = both_cores(rnd, x)
        if rnd in STRAIGHT:
            for k in (1, 3, 2):
                x_copy(rnd, k).wait_recv()
            mine = mine + x_recv[rnd, 0].astype(F32) + x_recv[rnd, 1].astype(F32)
        else:
            ring_copy(rnd, 2).wait_recv()
        acc[rnd] = mine + x_recv[rnd, 2].astype(F32)
        for ya in range(4):
            for za in range(4):
                y_sum[rnd, ya, pl.ds(za * LINE, LINE), :] = acc[rnd, pl.ds(za * UNIT + ya * LINE, LINE), :]
            y_sum[rnd, ya, pl.ds(UNIT, 8), :] = jnp.zeros((8, COL), F32)
        for k in (2, 1, 3):
            y_send[rnd, k - 1] = y_sum[rnd, lax.rem(y + k, 4)].astype(BF16)
            y_copy(rnd, k).start()

    def plane_copy(kx, ky):
        return pltpu.make_async_remote_copy(
            src_ref=p_send.at[kx * 4 + ky], dst_ref=p_recv.at[kx * 4 + ky],
            send_sem=p_sem.at[0], recv_sem=p_sem.at[1],
            device_id=device(zh, lax.rem(x + kx, 4), zl, lax.rem(y + ky, 4), c), device_id_type=MESH,
        )

    def plane(rnd):
        for kx in (2, 1, 3, 0):
            pair_copy(rnd, kx).wait_recv()
            p_acc[kx] = both_cores(rnd, lax.rem(x + kx, 4))
            for ya in range(4):
                for za in range(4):
                    p_sum[kx, ya, pl.ds(za * LINE, LINE), :] = p_acc[kx, pl.ds(za * UNIT + ya * LINE, LINE), :]
                p_sum[kx, ya, pl.ds(UNIT, 8), :] = jnp.zeros((8, COL), F32)
            for ky in (2, 1, 3, 0):
                if kx or ky:
                    p_send[kx * 4 + ky] = p_sum[kx, lax.rem(y + ky, 4)].astype(BF16)
                    plane_copy(kx, ky).start()

    def plane_wait():
        return pltpu.make_async_remote_copy(
            src_ref=p_send.at[pl.ds(1, 15)], dst_ref=p_recv.at[pl.ds(1, 15)],
            send_sem=p_sem.at[0], recv_sem=p_sem.at[1], device_id=sibling, device_id_type=MESH,
        )

    def z_copy(rnd, kz, kc):
        za = lax.rem(zh + kz, 4)
        ca = lax.rem(c + kc, 2)
        return pltpu.make_async_remote_copy(
            src_ref=z_send.at[rnd, za * 2 + ca], dst_ref=z_recv.at[rnd, kz * 2 + off],
            send_sem=z_ssem.at[rnd], recv_sem=z_rsem.at[rnd],
            device_id=device(za, x, c, y, ca), device_id_type=MESH,
        )

    def along_z(rnd):
        if rnd == LAST:
            plane_wait().wait_recv()
            z_sum[rnd] = p_sum[0, y] + jnp.sum(p_recv[pl.ds(1, 15)].astype(F32), axis=0)
        else:
            for k in (1, 3, 2):
                y_copy(rnd, k).wait_recv()
            z_sum[rnd] = (
                y_sum[rnd, y] + y_recv[rnd, 0].astype(F32)
                + y_recv[rnd, 1].astype(F32) + y_recv[rnd, 2].astype(F32)
            )
        for b in range(8):
            z_send[rnd, b] = z_sum[rnd, pl.ds(OWN * b, 16), :].astype(BF16)
        for kz in (2, 1, 3, 0):
            for kc in (1, 0):
                if kz == 0 and kc == 0:
                    @pl.when(off == 0)
                    def _():
                        z_recv[rnd, 0] = z_send[rnd, zh * 2 + c]
                    @pl.when(off == 1)
                    def _():
                        z_copy(rnd, 0, 0).start()
                else:
                    z_copy(rnd, kz, kc).start()

    def z_wait(rnd, recv):
        def wait(first):
            copy = pltpu.make_async_remote_copy(
                src_ref=z_send.at[rnd, pl.ds(first, 8 - first)],
                dst_ref=z_recv.at[rnd, pl.ds(first, 8 - first)],
                send_sem=z_ssem.at[rnd], recv_sem=z_rsem.at[rnd],
                device_id=sibling, device_id_type=MESH,
            )
            if recv:
                copy.wait_recv()
            else:
                copy.wait_send()
        @pl.when(off == 0)
        def _():
            wait(1)
        @pl.when(off == 1)
        def _():
            wait(0)

    def finish(rnd):
        z_wait(rnd, True)
        result = jnp.sum(z_recv[rnd].astype(F32), axis=0)[:OWN] * factor
        if rnd == PROJ:
            proj_ref[...] = result
        else:
            conv_ref[pl.ds(rnd, OWN, stride=CHUNKS), :] = result

    def projection():
        grad = dot(mid[pl.ds(0, BINS), :], g_v[0], 0, 0)
        for w in range(1, WIN):
            grad = grad + dot(mid[pl.ds(w * BINS, BINS), :], g_v[w], 0, 0)
        for j in range(C // COL):
            total[PROJ, pl.ds(j, BN, stride=C // COL), :] = grad[:, j * COL:(j + 1) * COL]

    def block_output():
        for w in range(WIN):
            rows = pl.ds(w * BINS, BINS)
            out_v[w] = (x_v[w].astype(F32) + dot(mid[rows, :], p_v[...])).astype(BF16)

    def outer_taps(ch):
        first = WIN - 1
        for w in range(WIN):
            wait_halo(dup_recv, dup_sem, ch, w)
            wait_halo(dlo_recv, dlo_sem, ch, w)
            clear_if(s < 2, dlo_recv, ch, w)
            clear_if(s >= 62, dup_recv, ch, w)
            if w < first - 1:
                continue
            rows = pl.ds(0, first * BINS) if w == first - 1 else pl.ds(w * BINS, BINS)
            both = jnp.concatenate([dup_recv[ch, rows, :], dlo_recv[ch, rows, :]], axis=1)
            for m in range(WIN):
                term = dot(act_t[pl.ds(m * BINS, BINS), rows], both)
                low, high = pl.ds(m * BINS, BINS), pl.ds(2 * C + m * BINS, BINS)
                if w == first - 1:
                    total[ch, low, :] = term[:, :COL]
                    total[ch, high, :] = term[:, COL:]
                else:
                    total[ch, low, :] = total[ch, low, :] + term[:, :COL]
                    total[ch, high, :] = total[ch, high, :] + term[:, COL:]

    def input_side(ch):
        cols = pl.ds(ch * COL, COL)
        for w in range(WIN):
            rows = pl.ds(w * BINS, BINS)
            term = (
                dot(dup_recv[ch, rows, :], w_v[0, :, cols], 1, 1)
                + dot(d_send[ch, rows, :], w_v[1, :, cols], 1, 1)
                + dot(dlo_recv[ch, rows, :], w_v[2, :, cols], 1, 1)
            )
            if ch:
                term = term + dact[rows, :]
            if ch < CHUNKS - 1:
                dact[rows, :] = term
            else:
                dx_v[w] = (g_v[w].astype(F32) + term * slope_x[rows, :]).astype(BF16)

    middle(0)
    send_products(2)
    centre_tap(0)
    middle(1)
    centre_tap(1)
    outer_taps(0)
    stage_a(0)
    input_side(0)
    ring(0, 0)
    middle(2)
    centre_tap(2)
    ring(0, 1)
    projection()
    stage_a(PROJ)
    block_output()
    straight(PROJ)
    ring(0, 2)
    outer_taps(1)
    stage_a(1)
    input_side(1)
    straight(1)
    outer_taps(2)
    stage_a(2)
    along_y(0)
    along_y(PROJ)
    plane(2)
    along_y(1)
    input_side(2)
    along_z(0)
    along_z(PROJ)
    along_z(1)
    along_z(2)
    finish(0)
    finish(PROJ)
    finish(1)

    for i, (ref, to) in enumerate(((u_send, upper), (v_send, lower), (d_send, upper), (d_send, lower))):
        pltpu.make_async_remote_copy(
            src_ref=ref, dst_ref=ref, send_sem=ph_send_sem.at[i], recv_sem=u_sem.at[0, 0],
            device_id=to, device_id_type=MESH,
        ).wait_send()
    for rnd in range(ROUNDS):
        for k in range(4):
            pair_copy(rnd, k).wait_send()
        if rnd == LAST:
            plane_wait().wait_send()
        else:
            for k in (1, 2, 3):
                x_copy(rnd, k).wait_send()
                y_copy(rnd, k).wait_send()
        z_wait(rnd, False)
    finish(LAST)


def write_out(*refs):
    *refs, sem = refs
    copies = [pltpu.make_async_copy(refs[i], refs[4 + i], sem.at[i]) for i in range(4)]
    for copy in copies:
        copy.start()
    for copy in copies:
        copy.wait()


def local(inputs, dilated_tap_weight, proj_weight, cotangent):
    total_rows = inputs.shape[0] * lax.axis_size("dp") * inputs.shape[1] * lax.axis_size("seq")
    factor = 1.0 / math.sqrt(total_rows)
    vm = pltpu.VMEM
    dma = pltpu.SemaphoreType.DMA
    halo = (CHUNKS, ROWS, COL)
    hbm = pl.BlockSpec(memory_space=pl.ANY)
    vmem = pl.BlockSpec(memory_space=pltpu.VMEM)
    results = pl.pallas_call(
        functools.partial(kernel, factor),
        out_shape=(
            vm(inputs.shape, BF16), vm(inputs.shape, BF16), vm((CHUNKS * OWN, COL), F32), vm((OWN, COL), F32),
        ),
        in_specs=[hbm] * 4,
        out_specs=(vmem,) * 4,
        scratch_shapes=[
            vm((WIN, BINS, C), BF16), vm((3, C, BN), BF16), vm((BN, C), BF16), vm((WIN, BINS, C), BF16),
            vm((ROWS, C), BF16), vm((C, ROWS), BF16), vm((ROWS, C), F32),
            vm((ROWS, BN), F32), vm((ROWS, BN), F32), vm((ROWS, BN), BF16), vm((ROWS, C), F32),
            vm(halo, BF16), vm(halo, BF16), vm(halo, BF16), vm(halo, BF16),
            vm(halo, BF16), vm(halo, BF16), vm(halo, BF16),
            vm((ROUNDS, ALL, COL), F32),
            vm((ROUNDS, 4 * PART, COL), BF16), vm((ROUNDS, 4 * PART, COL), BF16),
            vm((ROUNDS, 3, PART, COL), BF16), vm((ROUNDS, 3, PART, COL), BF16),
            vm((ROUNDS, PART, COL), F32),
            vm((ROUNDS, 4, UNIT + 8, COL), F32),
            vm((ROUNDS, 3, UNIT + 8, COL), BF16), vm((ROUNDS, 3, UNIT + 8, COL), BF16),
            vm((ROUNDS, UNIT + 8, COL), F32),
            vm((ROUNDS, 8, 16, COL), BF16), vm((ROUNDS, 8, 16, COL), BF16),
            vm((4, PART, COL), F32), vm((4, 4, UNIT + 8, COL), F32),
            vm((16, UNIT + 8, COL), BF16), vm((16, UNIT + 8, COL), BF16),
            dma((8,)), dma((4,)),
            dma((CHUNKS, WIN)), dma((CHUNKS, WIN)), dma((CHUNKS, WIN)), dma((CHUNKS, WIN)),
            dma((ROUNDS, 4)), dma((ROUNDS, 4)), dma((ROUNDS, 3)), dma((ROUNDS, 3)),
            dma((ROUNDS, 3)), dma((ROUNDS, 3)),
            dma((ROUNDS,)), dma((ROUNDS,)), dma((2,)),
        ],
        compiler_params=pltpu.CompilerParams(
            collective_id=0, has_side_effects=True, vmem_limit_bytes=44 * 1024 * 1024
        ),
        name="block",
    )(*[pltpu.with_memory_space_constraint(a, pltpu.HBM)
        for a in (inputs, dilated_tap_weight, proj_weight, cotangent)])
    results = [pltpu.with_memory_space_constraint(r, pltpu.VMEM) for r in results]
    return pl.pallas_call(
        write_out,
        out_shape=tuple(jax.ShapeDtypeStruct(r.shape, r.dtype) for r in results),
        in_specs=[vmem] * 4,
        out_specs=(hbm,) * 4,
        scratch_shapes=[dma((4,))],
        name="write_out",
    )(*results)


def solution(mesh):
    return jax.shard_map(
        local,
        mesh=mesh,
        in_specs=(P("dp", "seq", None), P(), P(), P("dp", "seq", None)),
        out_specs=(
            P("dp", "seq", None),
            P("dp", "seq", None),
            P(("dp", "seq"), None),
            P(("dp", "seq"), None),
        ),
        check_vma=False,
    )
```
